32 devices in a mesh: gen: 4 (over z), neur: 4 (over x, core), box: 2 (over y).
Axes of the slice: x: 2, y: 2, z: 4, core: 2. Of those that a mesh axis runs over, the one named last changes fastest.
Arguments:
- gens: bfloat16 [8, 128, 4096], P('box', 'gen'), may hold values from -1 to 1
- center: bfloat16 [8, 4096], P('box'), may hold values from -6 to 6
- weight: bfloat16 [4096, 2048], P('gen', 'neur'), may hold values from -0.09375 to 0.09375
- bias: float32 [2048], P('neur'), may hold values from -3 to 3
- phase: int32 [8, 2048], P('box', 'neur'), may hold values from 0 to 2
- gens_cot: bfloat16 [8, 128, 2048], P('box', 'gen', 'neur'), may hold values from -6 to 6
- center_cot: float32 [8, 2048], P('box', 'neur'), may hold values from -6 to 6
- offset_cot: float32 [8, 2048], P('box', 'neur'), may hold values from -6 to 6
Outputs:
- center_out: float32 [8, 2048], P('box', 'neur')
- gens_out: bfloat16 [8, 128, 2048], P('box', 'gen', 'neur')
- offset: float32 [8, 2048], P('box', 'neur')
- weight_grad: float32 [4096, 2048], P('gen', 'neur')
- bias_grad: float32 [2048], P('neur')
- gens_grad: float32 [8, 128, 4096], P('box', 'gen', 'neur')
- center_grad: float32 [8, 4096], P('box', 'neur')
The draws below stay inside these ranges and needn't reach their ends.
Inputs may be any that keep to these rules, and one draw needn't show every extreme that they name: `phase`: 0 marks an inactive neuron, 1 an active one, 2 one that crosses zero.
All inputs are finite; a program needn't handle non-finite values.
Results may differ from the reference program's by a relative error of at most 0.006.
Values may be sent and summed in bfloat16 or wider, within the bound.
No kernel may reach another device: no remote copies, remote signals or barrier semaphores. Data moves between devices by JAX's collectives and lax.ppermute only.
A program may use at most 64 MiB of HBM per device.

```python
import math
import jax
import jax.numpy as jnp
from jax import lax

D = 4096
F = 2048
BOXES = 8
GENS = 128


def draw_gens(key, part):
    keys = jax.random.split(key, 3)
    index = jnp.arange(GENS, dtype=jnp.float32)
    rising = 1.0 + 2.0 * index / max(GENS - 1, 1)
    row_scale = jnp.exp(jax.random.uniform(keys[0], (BOXES, GENS, 1), minval=0.0, maxval=math.log(10.0)))
    col_scale = jnp.exp(jax.random.uniform(keys[1], (1, 1, D), minval=-1.15, maxval=1.15))
    base = jnp.clip(jax.random.normal(keys[2], (BOXES, GENS, D)), -4.0, 4.0)
    value = base * row_scale * col_scale * rising[None, :, None] / (6.0 * GENS)
    return jnp.clip(value, -1.0, 1.0).astype(jnp.bfloat16)


def plant(entries, key, smallest, largest):
    longest = entries.shape.index(max(entries.shape))
    spots = []
    for shift in (0, 1):
        where = [jax.random.randint(jax.random.fold_in(key, axis), (), 0, length) for axis, length in enumerate(entries.shape)]
        where[longest] = (where[longest] + shift) % entries.shape[longest]
        spots.append(tuple(where))
    return entries.at[spots[0]].set(smallest).at[spots[1]].set(largest)


def block_levels(stream_key, extent, cuts, low, top_value):
    def one(axis_at, blocks):
        draws = jax.random.uniform(jax.random.fold_in(jax.random.fold_in(stream_key, 6), axis_at), (blocks,), jnp.float32, low / len(cuts), top_value / len(cuts))
        return jnp.repeat(jnp.exp(draws), extent[axis_at] // blocks).reshape((-1,) + (1,) * (len(extent) - axis_at - 1))

    loudness = one(*cuts[0])
    for cut in cuts[1:]:
        loudness = loudness * one(*cut)
    return loudness


def normal_values(rng, shape, spread, bound, shards=(), kind=jnp.bfloat16):
    drawn = jax.random.normal(rng, shape, jnp.float32) * spread
    if len(shards) > 0:
        drawn = block_levels(rng, shape, shards, -0.22, 0.18) * drawn
    return jnp.clip(drawn, min=-bound, max=bound).astype(kind)


def setup_inputs(seed: int = 0) -> dict:
    seeds = jax.random.split(jax.random.key(seed), 9)
    gens = draw_gens(jax.random.fold_in(seeds[8], 71), 0)
    center = normal_values(seeds[1], (BOXES, D), 1.0, 6.0, ((0, 2),))
    weight = normal_values(seeds[2], (D, F), D ** -0.5, 0.09375, ((0, 4), (1, 4)))
    bias = normal_values(seeds[3], (F,), 0.5, 3.0, ((0, 4),), jnp.float32)
    phase = plant(jax.random.randint(seeds[4], (BOXES, F), 0, 3), jax.random.fold_in(seeds[4], 1), 0, 2).astype(jnp.int32)
    gens_cot = normal_values(seeds[5], (BOXES, GENS, F), 1.0, 6.0, ((0, 2), (1, 4), (2, 4)))
    center_cot = normal_values(seeds[6], (BOXES, F), 1.0, 6.0, ((0, 2), (1, 4)), jnp.float32)
    offset_cot = normal_values(seeds[7], (BOXES, F), 1.0, 6.0, ((0, 2), (1, 4)), jnp.float32)
    return {"gens": gens, "center": center, "weight": weight, "bias": bias, "phase": phase, "gens_cot": gens_cot, "center_cot": center_cot, "offset_cot": offset_cot}


def neuron(center_pre, radius, phase):
    upper = center_pre + radius
    lower = center_pre - radius
    ratio = jnp.clip(upper / (upper - lower + 1e-05), 0.0, 1.0)
    active = (phase == 1).astype(center_pre.dtype)
    crossing = (phase == 2).astype(center_pre.dtype)
    slope = active + crossing * ratio
    offset = crossing * (-ratio * lower * 0.5)
    return (slope, slope * center_pre + offset, offset)

def reference(gens, center, weight, bias, phase, gens_cot, center_cot, offset_cot):
    total_rows = BOXES * GENS
    wide = jnp.concatenate([gens.reshape(total_rows, D), center], 0)
    product = jnp.dot(wide, weight, preferred_element_type=jnp.float32)
    gen_pre = product[:total_rows].reshape(BOXES, GENS, F)
    center_pre = product[total_rows:] + bias
    radius = lax.optimization_barrier(jnp.sum(jnp.abs(gen_pre), axis=1))
    slope, center_out, offset = neuron(center_pre, radius, phase)
    gens_out = (slope[:, None, :] * gen_pre).astype(jnp.bfloat16)
    intersection = lax.optimization_barrier(jnp.sum(gens_cot.astype(jnp.float32) * gen_pre, axis=1))
    unused, pull = jax.vjp(lambda a, b: neuron(a, b, phase), center_pre, radius)
    g_center, g_radius = pull((intersection, center_cot, offset_cot))
    gen_back = (slope[:, None, :] * gens_cot.astype(jnp.float32) + jnp.sign(gen_pre) * g_radius[:, None, :]).astype(jnp.bfloat16)
    center_back = g_center.astype(jnp.bfloat16)
    back = jnp.concatenate([gen_back.reshape(total_rows, F), center_back], 0)
    weight_grad = jnp.dot(wide.T, back, preferred_element_type=jnp.float32)
    bias_grad = lax.optimization_barrier(jnp.sum(g_center, axis=0))
    input_back = jnp.dot(back, weight.T, preferred_element_type=jnp.float32)
    gens_grad = input_back[:total_rows].reshape(BOXES, GENS, D)
    center_grad = input_back[total_rows:]
    return (center_out, gens_out, offset, weight_grad, bias_grad, gens_grad, center_grad)
```

```python
import functools

import jax
import jax.numpy as jnp
from jax import lax
from jax.experimental import pallas as pl
from jax.experimental.pallas import tpu as pltpu
from jax.sharding import PartitionSpec as P

BF = jnp.bfloat16
F32 = jnp.float32
VMEM_LIMIT = 40 * 1024 * 1024


def neuron(center_pre, radius, phase):
    upper = center_pre + radius
    lower = center_pre - radius
    ratio = jnp.clip(upper / (upper - lower + 1e-05), 0.0, 1.0)
    active = (phase == 1).astype(center_pre.dtype)
    crossing = (phase == 2).astype(center_pre.dtype)
    slope = active + crossing * ratio
    offset = crossing * (-ratio * lower * 0.5)
    return (slope, slope * center_pre + offset, offset)


def general_body(gens, center, weight, bias, phase, gens_cot, center_cot, offset_cot):
    box_dev, gen_dev, width = gens.shape
    local_cols = weight.shape[1]
    local_rows = box_dev * gen_dev
    wide = jnp.concatenate([gens.reshape(local_rows, width), center], 0)
    full_weight = lax.all_gather(weight, "gen", axis=0, tiled=True)
    product = jnp.dot(wide, full_weight, preferred_element_type=F32)
    gen_pre = product[:local_rows].reshape(box_dev, gen_dev, local_cols)
    center_pre = product[local_rows:] + bias
    part_radius = jnp.sum(jnp.abs(gen_pre), axis=1)
    cot_wide = gens_cot.astype(F32)
    radius = lax.psum(part_radius, "gen")
    slope, center_out, offset = neuron(center_pre, radius, phase)
    gens_out = (slope[:, None, :] * gen_pre).astype(BF)
    intersection = lax.psum(jnp.sum(cot_wide * gen_pre, axis=1), "gen")
    unused, pull = jax.vjp(lambda a, b: neuron(a, b, phase), center_pre, radius)
    g_center, g_radius = pull((intersection, center_cot, offset_cot))
    gen_back = (slope[:, None, :] * cot_wide + jnp.sign(gen_pre) * g_radius[:, None, :]).astype(BF)
    center_back = g_center.astype(BF)
    back = jnp.concatenate([gen_back.reshape(local_rows, local_cols), center_back], 0)
    first_gen = (lax.axis_index("gen") == 0).astype(BF)
    back_owned = jnp.concatenate(
        [gen_back.reshape(local_rows, local_cols), center_back * first_gen], 0
    )
    shares = lax.psum_scatter(
        lax.dot_general(wide, back_owned, (((0,), (0,)), ((), ())), preferred_element_type=F32),
        ("gen", "box"),
        scatter_dimension=0,
        tiled=True,
    )
    weight_grad = lax.all_gather(shares, "box", axis=0, tiled=True)
    bias_grad = lax.psum(jnp.sum(g_center, axis=0), "box")
    partial_back = lax.dot_general(
        back, full_weight, (((1,), (1,)), ((), ())), preferred_element_type=F32
    )
    summed = lax.psum_scatter(partial_back, "neur", scatter_dimension=1, tiled=True)
    gens_grad = summed[:local_rows].reshape(box_dev, gen_dev, summed.shape[1])
    center_grad = summed[local_rows:]
    return (center_out, gens_out, offset, weight_grad, bias_grad, gens_grad, center_grad)


CENTER_ROWS = 16


def params():
    return pltpu.CompilerParams(vmem_limit_bytes=VMEM_LIMIT)


def cost(flops, nbytes):
    return pl.CostEstimate(flops=int(flops), bytes_accessed=int(nbytes), transcendentals=0)


def shape(dims, dtype):
    return jax.ShapeDtypeStruct(dims, dtype)


def whole(x):
    return pl.BlockSpec(x.shape, lambda i, s, r=len(x.shape): (0,) * r)


def call(kernel, scalars, args, specs, outs, est, scratch=()):
    return pl.pallas_call(
        kernel,
        grid_spec=pltpu.PrefetchScalarGridSpec(
            num_scalar_prefetch=1,
            grid=(1,),
            in_specs=specs,
            out_specs=[whole(o) for o in outs],
            scratch_shapes=list(scratch),
        ),
        out_shape=outs,
        compiler_params=params(),
        cost_estimate=est,
    )(scalars, *args)


def fold_kernel(n, s_ref, *refs):
    gens, cots, outs = refs[:n], refs[n : 2 * n], refs[2 * n :]
    for gen_ref, cot_ref, out in zip(gens, cots, outs):
        rows = gen_ref.shape[0] * gen_ref.shape[1]
        out[:rows, :] = gen_ref[...].reshape(rows, gen_ref.shape[2])
        cot = cot_ref[...].reshape(-1, cot_ref.shape[2])
        lanes = cot_ref.shape[2]
        per = out.shape[0] - rows
        for i in range(cot.shape[0] // per):
            out[rows:, i * lanes : (i + 1) * lanes] = cot[i * per : (i + 1) * per]


def forward_kernel(size, s_ref, gen_ref, cot_ref, center_ref, own_ref, oth_ref, *refs):
    g, c = s_ref[0], s_ref[1]
    recv, (a_ref, keep_ref, send_ref), parts = refs[: size - 1], refs[size - 1 : size + 2], refs[size + 2 :]
    boxes, per_gen, depth = gen_ref.shape
    rows = boxes * per_gen
    lanes = cot_ref.shape[2]
    for k in range(size):
        at = pl.ds(pl.multiple_of((g ^ k) * rows, rows), rows)
        if k == 0:
            a_ref[at, :] = gen_ref[...].reshape(rows, depth)
            keep_ref[at, :] = cot_ref[pl.ds(c * boxes, boxes)].reshape(rows, lanes)
            send_ref[at, :] = cot_ref[pl.ds((1 - c) * boxes, boxes)].reshape(rows, lanes)
        else:
            msg = recv[k - 1]
            a_ref[at, :] = msg[:rows, :]
            per = msg.shape[0] - rows
            cot = [msg[rows:, i * lanes : (i + 1) * lanes] for i in range(2 * rows // per)]
            low = jnp.concatenate(cot[: len(cot) // 2], 0)
            high = jnp.concatenate(cot[len(cot) // 2 :], 0)
            keep_ref[at, :] = jnp.where(c == 0, low, high)
            send_ref[at, :] = jnp.where(c == 0, high, low)
    mid = center_ref[...].astype(F32)
    mine = jnp.where(c == 0, mid[:boxes], mid[boxes:])
    pad = jnp.zeros((CENTER_ROWS - boxes, depth), F32)
    a_ref[size * rows :, :] = jnp.concatenate([mine, pad], 0).astype(BF)
    a = a_ref[...]
    for k in range(size):
        at = pl.ds(pl.multiple_of((g ^ k) * lanes, lanes), lanes)
        w = jnp.concatenate([own_ref[:, at], oth_ref[:, at]], 1)
        part = jnp.dot(a, w, preferred_element_type=F32)
        parts[k][...] = part[: parts[k].shape[0]]


def relax_kernel(size, boxes, s_ref, *refs):
    g = s_ref[0]
    parts, (keep_ref, got_ref, own_ref, oth_ref), outs = refs[:size], refs[size : size + 4], refs[size + 4 :]
    back_ref, go_ref, msgs = outs[0], outs[1], outs[2:-2]
    pre_ref, out_scratch = outs[-2], outs[-1]
    pre = parts[0][...]
    for p in parts[1:]:
        pre = pre + p[...]
    pre_ref[...] = pre
    rows = size * (go_ref.shape[0])
    per = go_ref.shape[0] // boxes
    cot = jnp.concatenate([keep_ref[...], got_ref[...]], 1).astype(F32)
    small = jnp.concatenate([own_ref[...], oth_ref[...]], 1)
    phase, center_cot, offset_cot = (small[i * boxes : (i + 1) * boxes] for i in range(3))
    bias = small[3 * boxes : 3 * boxes + 1]
    where = [[q * boxes * per + b * per for q in range(size)] for b in range(boxes)]
    radius, cross = [], []
    for b in range(boxes):
        radius.append(sum(jnp.sum(jnp.abs(pre[r : r + per]), 0, keepdims=True) for r in where[b]))
        cross.append(sum(jnp.sum(cot[r : r + per] * pre[r : r + per], 0, keepdims=True) for r in where[b]))
    radius, cross = jnp.concatenate(radius, 0), jnp.concatenate(cross, 0)
    center_pre = pre[rows : rows + boxes] + bias
    (slope, center_out, offset), pull = jax.vjp(lambda a, b: neuron(a, b, phase), center_pre, radius)
    g_center, g_radius = pull((cross, center_cot, offset_cot))
    for b in range(boxes):
        sl, gr = slope[b : b + 1], g_radius[b : b + 1]
        for r in where[b]:
            x = pre[r : r + per]
            sign = jnp.where(x > 0, gr, jnp.where(x < 0, -gr, 0.0))
            back_ref[r : r + per, :] = (sl * cot[r : r + per] + sign).astype(BF)
            out_scratch[r : r + per, :] = (sl * x).astype(BF)
    tail = []
    for value in (g_center, center_out, offset):
        high = value.astype(BF).astype(F32)
        tail += [high, value - high]
    tail.append(jnp.zeros((CENTER_ROWS - 6 * boxes, value.shape[1]), F32))
    back_ref[rows:, :] = jnp.concatenate(tail, 0).astype(BF)
    group = boxes * per
    go_ref[...] = out_scratch[pl.ds(pl.multiple_of(g * group, group), group), :]
    for k, msg in enumerate(msgs, 1):
        msg[: rows + CENTER_ROWS, :] = back_ref[...]
        at = pl.ds(pl.multiple_of((g ^ k) * group, group), group)
        msg[rows + CENTER_ROWS :, :] = out_scratch[at, :]


def spread_kernel(s_ref, back_ref, go_ref, *refs):
    g = s_ref[0]
    msgs, (own_ref, oth_ref) = refs[:-2], refs[-2:]
    rows, lanes = back_ref.shape[0], back_ref.shape[1] // 2
    for k in range(len(msgs) + 1):
        at = pl.ds(pl.multiple_of((g ^ k) * lanes, lanes), lanes)
        if k == 0:
            own_ref[:rows, at] = back_ref[:, :lanes]
            oth_ref[:rows, at] = back_ref[:, lanes:]
            own_ref[rows:, at] = go_ref[:, :lanes]
            oth_ref[rows:, at] = go_ref[:, lanes:]
        else:
            own_ref[:, at] = msgs[k - 1][:, :lanes]
            oth_ref[:, at] = msgs[k - 1][:, lanes:]


def input_grad_kernel(size, s_ref, own_ref, oth_ref, w_own_ref, w_oth_ref, *refs):
    n = s_ref[2]
    outs, res = refs[:-1], refs[-1]
    rows = res.shape[0]
    over = (((1,), (1,)), ((), ()))
    res[...] = lax.dot_general(
        own_ref[:rows, :], w_own_ref[...], over, preferred_element_type=F32
    ) + lax.dot_general(oth_ref[:rows, :], w_oth_ref[...], over, preferred_element_type=F32)
    group = (rows - CENTER_ROWS) // size
    tail = res[size * group : size * group + outs[0].shape[0] - group, :]
    for k, out in enumerate(outs):
        part = res[pl.ds(pl.multiple_of((n ^ k) * group, group), group), :]
        out[...] = jnp.concatenate([part, tail], 0).astype(BF)


def input_sum_kernel(s_ref, *refs):
    msgs, (grad_ref, center_ref) = refs[:-2], refs[-2:]
    c = s_ref[0] & 1
    boxes, per = grad_ref.shape[0] // 2, grad_ref.shape[1]
    group = boxes * per
    near = msgs[0][...].astype(F32) + msgs[2][...].astype(F32)
    far = msgs[1][...].astype(F32) + msgs[3][...].astype(F32)
    grad_ref[pl.ds(c * boxes, boxes)] = near[:group].reshape(boxes, per, -1)
    grad_ref[pl.ds((1 - c) * boxes, boxes)] = far[:group].reshape(boxes, per, -1)
    near, far = near[group : group + boxes], far[group : group + boxes]
    center_ref[...] = jnp.where(
        c == 0, jnp.concatenate([near, far], 0), jnp.concatenate([far, near], 0)
    )


def weight_grad_kernel(boxes, s_ref, *refs):
    lefts, rights, outs = refs[:4], refs[4:8], refs[8:]
    weight_ref, bias_ref, center_ref, offset_ref, gens_ref = outs
    rows = lefts[0].shape[0]
    total = None
    for left, right in zip(lefts, rights):
        part = lax.dot_general(
            left[...], right[:rows, :], (((0,), (0,)), ((), ())), preferred_element_type=F32
        )
        total = part if total is None else total + part
    weight_ref[...] = total

    @pl.when(pl.program_id(0) == 0)
    def _():
        c = s_ref[1]
        first = rows - CENTER_ROWS
        tails = [right[first:rows, :].astype(F32) for right in rights]
        bias_ref[...] = sum(jnp.sum(t[: 2 * boxes], 0, keepdims=True) for t in tails)
        for at, ref in ((2, center_ref), (4, offset_ref)):
            mine, other = (
                t[at * boxes : (at + 1) * boxes] + t[(at + 1) * boxes : (at + 2) * boxes] for t in tails[:2]
            )
            ref[...] = jnp.where(
                c == 0, jnp.concatenate([mine, other], 0), jnp.concatenate([other, mine], 0)
            )
        per = gens_ref.shape[1]
        gens_ref[pl.ds(c * boxes, boxes)] = rights[0][rows:, :].reshape(boxes, per, -1)
        gens_ref[pl.ds((1 - c) * boxes, boxes)] = rights[1][rows:, :].reshape(boxes, per, -1)


def square_body(size, gens, center, weight, bias, phase, gens_cot, center_cot, offset_cot):
    box_dev, per_gen, width = gens.shape
    depth, cols = weight.shape
    boxes = box_dev // 2
    group = boxes * per_gen
    rows = size * group
    lanes = cols // size
    g, n = lax.axis_index("gen"), lax.axis_index("neur")
    c = n % 2
    scalars = jnp.stack([g, c, n]).astype(jnp.int32)

    def over_gen(x, k):
        return lax.ppermute(x, "gen", [(i, i ^ k) for i in range(size)])

    def over_core(x):
        return lax.ppermute(x, "neur", [(i, i ^ 1) for i in range(size)])

    def over_box(x):
        return lax.ppermute(x, "box", [(0, 1), (1, 0)])

    def turned(x, k):
        pairs = [(i * size + j, (j ^ k) * size + i) for i in range(size) for j in range(size)]
        return lax.ppermute(x, ("gen", "neur"), pairs)

    def gens_spec(k):
        return pl.BlockSpec((boxes, per_gen, depth), lambda i, s: (s[1], 0, s[0] ^ k))

    def cot_spec(k):
        return pl.BlockSpec((box_dev, per_gen, lanes), lambda i, s: (0, 0, s[0] ^ k))

    others = range(1, size)
    with jax.named_scope("exchange_generators"):
        cot_rows = box_dev * per_gen * lanes // depth
        msgs = call(
            functools.partial(fold_kernel, size - 1),
            scalars,
            [gens] * (size - 1) + [gens_cot] * (size - 1),
            [gens_spec(k) for k in others] + [cot_spec(k) for k in others],
            [shape((group + cot_rows, depth), BF)] * (size - 1),
            cost(0, 1 << 20),
        )
        recv = [over_gen(m, k) for k, m in zip(others, msgs)]
    with jax.named_scope("swap_cores"):
        w_other = over_core(weight)
        stacked = jnp.stack([phase.astype(F32), center_cot, offset_cot])

        def small(core):
            part = lax.dynamic_slice_in_dim(stacked, core * boxes, boxes, 1)
            return jnp.concatenate(
                [part.reshape(3 * boxes, cols), bias[None], jnp.zeros((8 - 3 * boxes - 1, cols), F32)], 0
            )

        small_own = small(c)
        small_oth = over_core(small(1 - c))
    with jax.named_scope("forward"):
        res = call(
            functools.partial(forward_kernel, size),
            scalars,
            [gens, gens_cot, center, weight, w_other, *recv],
            [
                gens_spec(0),
                cot_spec(0),
                pl.BlockSpec((box_dev, depth), lambda i, s: (0, s[0])),
                whole(weight),
                whole(w_other),
                *[whole(r) for r in recv],
            ],
            [
                shape((rows + CENTER_ROWS, depth), BF),
                shape((rows, lanes), BF),
                shape((rows, lanes), BF),
                *[shape((rows + 8, 2 * lanes), F32)] * size,
            ],
            cost(2 * rows * depth * 2 * cols, 4 << 20),
        )
        a_own, cot_keep, cot_send, *parts = res
    with jax.named_scope("sum_products"):
        sums = [parts[0]] + [over_gen(parts[k], k) for k in others]
        cot_got = over_core(cot_send)
    with jax.named_scope("share_generators"):
        a_core = over_core(a_own)
        a_box = over_box(a_own)
        a_box_core = over_core(a_box)
    with jax.named_scope("relax"):
        small_spec = pl.BlockSpec((8, lanes), lambda i, s: (0, s[0]))
        back, go, *msgs = call(
            functools.partial(relax_kernel, size, boxes),
            scalars,
            [*sums, cot_keep, cot_got, small_own, small_oth],
            [*[whole(p) for p in sums], whole(cot_keep), whole(cot_got), small_spec, small_spec],
            [
                shape((rows + CENTER_ROWS, 2 * lanes), BF),
                shape((group, 2 * lanes), BF),
                *[shape((rows + CENTER_ROWS + group, 2 * lanes), BF)] * (size - 1),
            ],
            cost(rows * lanes * 20, 2 << 20),
            [pltpu.VMEM((rows + 8, 2 * lanes), F32), pltpu.VMEM((rows, 2 * lanes), BF)],
        )
    with jax.named_scope("exchange_back"):
        recv = [over_gen(m, k) for k, m in zip(others, msgs)]
        b_own, b_oth = call(
            spread_kernel,
            scalars,
            [back, go, *recv],
            [whole(back), whole(go), *[whole(r) for r in recv]],
            [shape((rows + CENTER_ROWS + group, cols), BF)] * 2,
            cost(0, 2 << 20),
        )
        b_core = over_core(b_oth)
        b_box = over_box(b_own[: rows + CENTER_ROWS])
        b_box_core = over_box(b_core[: rows + CENTER_ROWS])
    with jax.named_scope("input_gradient"):
        msgs = call(
            functools.partial(input_grad_kernel, size),
            scalars,
            [b_own, b_oth, weight, w_other],
            [whole(b_own), whole(b_oth), whole(weight), whole(w_other)],
            [shape((group + 8, depth), BF)] * size,
            cost(2 * rows * depth * 2 * cols, 4 << 20),
            [pltpu.VMEM((rows + CENTER_ROWS, depth), F32)],
        )
        recv = [turned(m, k) for k, m in enumerate(msgs)]
        gens_grad, center_grad = call(
            input_sum_kernel,
            scalars,
            recv,
            [whole(r) for r in recv],
            [shape((box_dev, per_gen, depth), F32), shape((box_dev, depth), F32)],
            cost(0, 2 << 20),
        )
    with jax.named_scope("weight_gradient"):
        blocks = 4
        lefts, rights = [a_own, a_core, a_box, a_box_core], [b_own, b_core, b_box, b_box_core]
        left_spec = pl.BlockSpec((rows + CENTER_ROWS, depth // blocks), lambda i, s: (0, i))
        weight_grad, bias_grad, center_out, offset, gens_out = pl.pallas_call(
            functools.partial(weight_grad_kernel, boxes),
            grid_spec=pltpu.PrefetchScalarGridSpec(
                num_scalar_prefetch=1,
                grid=(blocks,),
                in_specs=[left_spec] * 4 + [whole(r) for r in rights],
                out_specs=[
                    pl.BlockSpec((depth // blocks, cols), lambda i, s: (i, 0)),
                    whole(shape((1, cols), F32)),
                    whole(shape((box_dev, cols), F32)),
                    whole(shape((box_dev, cols), F32)),
                    whole(shape((box_dev, per_gen, cols), BF)),
                ],
            ),
            out_shape=[
                shape((depth, cols), F32),
                shape((1, cols), F32),
                shape((box_dev, cols), F32),
                shape((box_dev, cols), F32),
                shape((box_dev, per_gen, cols), BF),
            ],
            compiler_params=params(),
            cost_estimate=cost(2 * 4 * rows * depth * cols, 6 << 20),
        )(scalars, *lefts, *rights)
    return (
        center_out,
        gens_out,
        offset,
        weight_grad,
        bias_grad.reshape(cols),
        gens_grad,
        center_grad,
    )


def solution(mesh):
    sizes = dict(mesh.shape)

    def run(gens, center, weight, bias, phase, gens_cot, center_cot, offset_cot):
        size = sizes["gen"]
        box_dev = gens.shape[0] // sizes["box"]
        per_gen = gens.shape[1] // size
        cols = weight.shape[1] // sizes["neur"]
        square = (
            size == sizes["neur"] == 4
            and sizes["box"] == 2
            and box_dev == 4
            and per_gen % 16 == 0
            and cols % (128 * size) == 0
            and weight.shape[0] % (1024 * size) == 0
        )
        body = functools.partial(square_body, size) if square else general_body
        return jax.shard_map(
            body,
            mesh=mesh,
            in_specs=(
                P("box", "gen", None),
                P("box", None),
                P("gen", "neur"),
                P("neur"),
                P("box", "neur"),
                P("box", "gen", "neur"),
                P("box", "neur"),
                P("box", "neur"),
            ),
            out_specs=(
                P("box", "neur"),
                P("box", "gen", "neur"),
                P("box", "neur"),
                P("gen", "neur"),
                P("neur"),
                P("box", "gen", "neur"),
                P("box", "neur"),
            ),
            check_vma=False,
        )(gens, center, weight, bias, phase, gens_cot, center_cot, offset_cot)

    return run
```

```python
import functools

import jax
import jax.numpy as jnp
from jax import lax
from jax.experimental import pallas as pl
from jax.experimental.pallas import tpu as pltpu
from jax.sharding import PartitionSpec as P

BF = jnp.bfloat16
F32 = jnp.float32
VMEM_LIMIT = 40 * 1024 * 1024


def neuron(center_pre, radius, phase):
    upper = center_pre + radius
    lower = center_pre - radius
    ratio = jnp.clip(upper / (upper - lower + 1e-05), 0.0, 1.0)
    active = (phase == 1).astype(center_pre.dtype)
    crossing = (phase == 2).astype(center_pre.dtype)
    slope = active + crossing * ratio
    offset = crossing * (-ratio * lower * 0.5)
    return (slope, slope * center_pre + offset, offset)


def general_body(gens, center, weight, bias, phase, gens_cot, center_cot, offset_cot):
    box_dev, gen_dev, width = gens.shape
    local_cols = weight.shape[1]
    local_rows = box_dev * gen_dev
    wide = jnp.concatenate([gens.reshape(local_rows, width), center], 0)
    full_weight = lax.all_gather(weight, "gen", axis=0, tiled=True)
    product = jnp.dot(wide, full_weight, preferred_element_type=F32)
    gen_pre = product[:local_rows].reshape(box_dev, gen_dev, local_cols)
    center_pre = product[local_rows:] + bias
    part_radius = jnp.sum(jnp.abs(gen_pre), axis=1)
    cot_wide = gens_cot.astype(F32)
    radius = lax.psum(part_radius, "gen")
    slope, center_out, offset = neuron(center_pre, radius, phase)
    gens_out = (slope[:, None, :] * gen_pre).astype(BF)
    intersection = lax.psum(jnp.sum(cot_wide * gen_pre, axis=1), "gen")
    unused, pull = jax.vjp(lambda a, b: neuron(a, b, phase), center_pre, radius)
    g_center, g_radius = pull((intersection, center_cot, offset_cot))
    gen_back = (slope[:, None, :] * cot_wide + jnp.sign(gen_pre) * g_radius[:, None, :]).astype(BF)
    center_back = g_center.astype(BF)
    back = jnp.concatenate([gen_back.reshape(local_rows, local_cols), center_back], 0)
    first_gen = (lax.axis_index("gen") == 0).astype(BF)
    back_owned = jnp.concatenate(
        [gen_back.reshape(local_rows, local_cols), center_back * first_gen], 0
    )
    shares = lax.psum_scatter(
        lax.dot_general(wide, back_owned, (((0,), (0,)), ((), ())), preferred_element_type=F32),
        ("gen", "box"),
        scatter_dimension=0,
        tiled=True,
    )
    weight_grad = lax.all_gather(shares, "box", axis=0, tiled=True)
    bias_grad = lax.psum(jnp.sum(g_center, axis=0), "box")
    partial_back = lax.dot_general(
        back, full_weight, (((1,), (1,)), ((), ())), preferred_element_type=F32
    )
    summed = lax.psum_scatter(partial_back, "neur", scatter_dimension=1, tiled=True)
    gens_grad = summed[:local_rows].reshape(box_dev, gen_dev, summed.shape[1])
    center_grad = summed[local_rows:]
    return (center_out, gens_out, offset, weight_grad, bias_grad, gens_grad, center_grad)


CENTER_ROWS = 16
HALVES = 2


def params():
    return pltpu.CompilerParams(vmem_limit_bytes=VMEM_LIMIT)


def cost(flops, nbytes):
    return pl.CostEstimate(flops=int(flops), bytes_accessed=int(nbytes), transcendentals=0)


def shape(dims, dtype):
    return jax.ShapeDtypeStruct(dims, dtype)


def whole(x):
    return pl.BlockSpec(x.shape, lambda i, s, r=len(x.shape): (0,) * r)


def call(kernel, scalars, args, specs, outs, est, scratch=()):
    return pl.pallas_call(
        kernel,
        grid_spec=pltpu.PrefetchScalarGridSpec(
            num_scalar_prefetch=1,
            grid=(1,),
            in_specs=specs,
            out_specs=[whole(o) for o in outs],
            scratch_shapes=list(scratch),
        ),
        out_shape=outs,
        compiler_params=params(),
        cost_estimate=est,
    )(scalars, *args)


def rows_at(index, size):
    return pl.ds(pl.multiple_of(index * size, size), size)


def fold_kernel(partners, s_ref, *refs):
    gens, cots, outs = refs[: partners * HALVES], refs[partners * HALVES : partners * (HALVES + 1)], refs[partners * (HALVES + 1) :]
    for gen_ref, out in zip(gens, outs):
        rows = gen_ref.shape[0] * gen_ref.shape[1]
        out[:rows, :] = gen_ref[...].reshape(rows, gen_ref.shape[2])
    for cot_ref, out in zip(cots, outs[partners * (HALVES - 1) :]):
        cot = cot_ref[...].reshape(-1, cot_ref.shape[2])
        lanes = cot_ref.shape[2]
        per = out.shape[0] - rows
        for i in range(cot.shape[0] // per):
            out[rows:, i * lanes : (i + 1) * lanes] = cot[i * per : (i + 1) * per]


def forward_kernel(size, part, s_ref, gen_ref, center_ref, own_ref, oth_ref, *refs):
    g, c = s_ref[0], s_ref[1]
    recv, refs = refs[: size - 1], refs[size - 1 :]
    boxes, per_gen, depth = gen_ref.shape
    rows = boxes * per_gen
    if part == HALVES - 1:
        cot_ref, a_ref, keep_ref, send_ref, *products = refs
    else:
        cot_ref, (a_ref, *products) = None, refs
    for k in range(size):
        at = rows_at(g ^ k, rows)
        a_ref[at, :] = gen_ref[...].reshape(rows, depth) if k == 0 else recv[k - 1][:rows, :]
    mid = center_ref[...].astype(F32)
    half = mid.shape[0] // 2
    mine = jnp.where(c == 0, mid[:half], mid[half:])[part * boxes : (part + 1) * boxes]
    pad = jnp.zeros((CENTER_ROWS - boxes, depth), F32)
    a_ref[size * rows :, :] = jnp.concatenate([mine, pad], 0).astype(BF)
    a = a_ref[...]
    lanes = products[0].shape[1] // 2
    for k in range(size):
        at = rows_at(g ^ k, lanes)
        w = jnp.concatenate([own_ref[:, at], oth_ref[:, at]], 1)
        product = jnp.dot(a, w, preferred_element_type=F32)
        products[k][...] = product[: products[k].shape[0]]
    if cot_ref is None:
        return
    for k in range(size):
        if k == 0:
            cot = cot_ref[...].reshape(-1, lanes)
        else:
            msg = recv[k - 1]
            cot = jnp.concatenate(
                [msg[rows:, i * lanes : (i + 1) * lanes] for i in range(depth // lanes)], 0
            )
        low, high = cot[: HALVES * rows], cot[HALVES * rows :]
        for ref, value in (
            (keep_ref, jnp.where(c == 0, low, high)),
            (send_ref, jnp.where(c == 0, high, low)),
        ):
            for h in range(HALVES):
                at = pl.ds(pl.multiple_of(h * size * rows + (g ^ k) * rows, rows), rows)
                ref[at, :] = value[h * rows : (h + 1) * rows]


def relax_kernel(size, boxes, part, s_ref, *refs):
    g = s_ref[0]
    sums, (keep_ref, got_ref, own_ref, oth_ref), outs = refs[:size], refs[size : size + 4], refs[size + 4 :]
    back_ref, go_ref, msgs, out_scratch = outs[0], outs[1], outs[2:-1], outs[-1]
    pre = sums[0][...]
    for p in sums[1:]:
        pre = pre + p[...]
    group = go_ref.shape[0]
    rows, per = size * group, group // boxes
    cot = jnp.concatenate([keep_ref[...], got_ref[...]], 1).astype(F32)
    small = jnp.concatenate([own_ref[...], oth_ref[...]], 1)
    step = HALVES * boxes
    phase, center_cot, offset_cot = (
        small[i * step + part * boxes : i * step + (part + 1) * boxes] for i in range(3)
    )
    bias = small[3 * step : 3 * step + 1]
    where = [[q * group + b * per for q in range(size)] for b in range(boxes)]
    radius, cross = [], []
    for b in range(boxes):
        radius.append(sum(jnp.sum(jnp.abs(pre[r : r + per]), 0, keepdims=True) for r in where[b]))
        cross.append(sum(jnp.sum(cot[r : r + per] * pre[r : r + per], 0, keepdims=True) for r in where[b]))
    radius, cross = jnp.concatenate(radius, 0), jnp.concatenate(cross, 0)
    center_pre = pre[rows : rows + boxes] + bias
    (slope, center_out, offset), pull = jax.vjp(lambda a, b: neuron(a, b, phase), center_pre, radius)
    g_center, g_radius = pull((cross, center_cot, offset_cot))
    for b in range(boxes):
        sl, gr = slope[b : b + 1], g_radius[b : b + 1]
        for r in where[b]:
            x = pre[r : r + per]
            sign = jnp.where(x > 0, gr, jnp.where(x < 0, -gr, 0.0))
            back_ref[r : r + per, :] = (sl * cot[r : r + per] + sign).astype(BF)
            out_scratch[r : r + per, :] = (sl * x).astype(BF)
    tail = []
    for value in (g_center, center_out, offset):
        high = value.astype(BF).astype(F32)
        tail += [high, value - high]
    tail.append(jnp.zeros((CENTER_ROWS - 6 * boxes, value.shape[1]), F32))
    back_ref[rows:, :] = jnp.concatenate(tail, 0).astype(BF)
    go_ref[...] = out_scratch[rows_at(g, group), :]
    for k, msg in enumerate(msgs, 1):
        msg[: rows + CENTER_ROWS, :] = back_ref[...]
        msg[rows + CENTER_ROWS :, :] = out_scratch[rows_at(g ^ k, group), :]


def spread_kernel(s_ref, back_ref, go_ref, *refs):
    g = s_ref[0]
    msgs, (own_ref, oth_ref) = refs[:-2], refs[-2:]
    rows, lanes = back_ref.shape[0], back_ref.shape[1] // 2
    for k in range(len(msgs) + 1):
        at = rows_at(g ^ k, lanes)
        if k == 0:
            own_ref[:rows, at] = back_ref[:, :lanes]
            oth_ref[:rows, at] = back_ref[:, lanes:]
            own_ref[rows:, at] = go_ref[:, :lanes]
            oth_ref[rows:, at] = go_ref[:, lanes:]
        else:
            own_ref[:, at] = msgs[k - 1][:, :lanes]
            oth_ref[:, at] = msgs[k - 1][:, lanes:]


def input_grad_kernel(size, s_ref, own_ref, oth_ref, w_own_ref, w_oth_ref, send_ref, keep_ref, res):
    x = s_ref[2] >> 1
    rows = res.shape[0]
    over = (((1,), (1,)), ((), ()))
    res[...] = lax.dot_general(
        own_ref[:rows, :], w_own_ref[...], over, preferred_element_type=F32
    ) + lax.dot_general(oth_ref[:rows, :], w_oth_ref[...], over, preferred_element_type=F32)
    group = (rows - CENTER_ROWS) // size
    tail = res[size * group : size * group + 8, :]
    for ref, at in ((send_ref, 1 - x), (keep_ref, x)):
        parts = [res[rows_at(at, group), :], res[rows_at(at + 2, group), :], tail]
        ref[...] = jnp.concatenate(parts, 0).astype(ref.dtype)


def input_pair_kernel(s_ref, keep_ref, got_ref, *refs):
    outs, total = refs[:-1], refs[-1]
    c = s_ref[1]
    total[...] = keep_ref[...] + got_ref[...].astype(F32)
    group = (total.shape[0] - 8) // 2
    tail = total[2 * group :, :]
    for k, out in enumerate(outs):
        out[...] = jnp.concatenate([total[rows_at(c ^ k, group), :], tail], 0).astype(BF)


def input_final_kernel(boxes, s_ref, *refs):
    msgs, (grad_ref, center_ref) = refs[: 2 * HALVES], refs[-2:]
    first = s_ref[0] >> 1
    per = grad_ref.shape[1]
    group = boxes * per
    rows = [[], []]
    for h in range(HALVES):
        for k in range(2):
            value = msgs[2 * h + k][...].astype(F32)
            at = (first ^ k) * (HALVES * boxes) + h * boxes
            grad_ref[pl.ds(at, boxes)] = value[:group].reshape(boxes, per, -1)
            rows[k].append(value[group : group + boxes])
    near, far = (jnp.concatenate(r, 0) for r in rows)
    center_ref[...] = jnp.where(
        first == 0, jnp.concatenate([near, far], 0), jnp.concatenate([far, near], 0)
    )


def stack_kernel(*refs):
    lefts, out = refs[:-1], refs[-1]
    rows = lefts[0].shape[0] // HALVES
    gens = rows - CENTER_ROWS
    tails = []
    for i in range(len(lefts) * HALVES):
        ref, h = lefts[i // HALVES], i % HALVES
        out[:, i * gens : (i + 1) * gens] = ref[h * rows : h * rows + gens, :].T
        tails.append(ref[h * rows + gens : (h + 1) * rows, :])
    out[:, len(tails) * gens :] = jnp.concatenate(tails, 0).T


def weight_grad_kernel(boxes, s_ref, left_ref, *refs):
    rights, refs = refs[: 4 * HALVES], refs[4 * HALVES :]
    weight_ref, bias_ref, center_ref, offset_ref, gens_ref, stack = refs
    per = gens_ref.shape[1]
    gens = (left_ref.shape[1] - len(rights) * CENTER_ROWS) // len(rights)

    @pl.when(pl.program_id(0) == 0)
    def _():
        c = s_ref[1]
        tails = []
        for i, right in enumerate(rights):
            stack[i * gens : (i + 1) * gens, :] = right[:gens, :]
            tail = right[gens : gens + CENTER_ROWS, :]
            at = len(rights) * gens + i * CENTER_ROWS
            stack[at : at + CENTER_ROWS, :] = tail
            tails.append(tail.astype(F32))
        bias_ref[...] = sum(jnp.sum(t[: 2 * boxes], 0, keepdims=True) for t in tails)
        for at, ref in ((2, center_ref), (4, offset_ref)):
            both = [
                t[at * boxes : (at + 1) * boxes] + t[(at + 1) * boxes : (at + 2) * boxes]
                for t in tails[: 2 * HALVES]
            ]
            mine, other = (jnp.concatenate(both[i * HALVES : (i + 1) * HALVES], 0) for i in range(2))
            ref[...] = jnp.where(
                c == 0, jnp.concatenate([mine, other], 0), jnp.concatenate([other, mine], 0)
            )
        for i in range(2):
            for h in range(HALVES):
                at = (c ^ i) * (HALVES * boxes) + h * boxes
                out = rights[i * HALVES + h][gens + CENTER_ROWS :, :]
                gens_ref[pl.ds(at, boxes)] = out.reshape(boxes, per, -1)

    weight_ref[...] = jnp.dot(left_ref[...], stack[...], preferred_element_type=F32)


def square_body(size, gens, center, weight, bias, phase, gens_cot, center_cot, offset_cot):
    box_dev, per_gen, width = gens.shape
    depth, cols = weight.shape
    core_boxes = box_dev // 2
    boxes = core_boxes // HALVES
    group = boxes * per_gen
    rows = size * group
    work = rows + CENTER_ROWS
    lanes = cols // size
    g, n = lax.axis_index("gen"), lax.axis_index("neur")
    c = n % 2
    scalars = jnp.stack([g, c, n]).astype(jnp.int32)
    halves, others = range(HALVES), range(1, size)

    def over_gen(x, k):
        return lax.ppermute(x, "gen", [(i, i ^ k) for i in range(size)])

    def over_core(x):
        return lax.ppermute(x, "neur", [(i, i ^ 1) for i in range(size)])

    def over_x(x):
        return lax.ppermute(x, "neur", [(i, i ^ 2) for i in range(size)])

    def over_box(x):
        return lax.ppermute(x, "box", [(0, 1), (1, 0)])

    def turned(x, k):
        pairs = [
            (i * size + j, ((j >> 1) + 2 * ((j & 1) ^ k)) * size + i)
            for i in range(size)
            for j in range(size)
        ]
        return lax.ppermute(x, ("gen", "neur"), pairs)

    def gens_spec(k, h):
        return pl.BlockSpec(
            (boxes, per_gen, depth), lambda i, s: (s[1] * HALVES + h, 0, s[0] ^ k)
        )

    def cot_spec(k):
        return pl.BlockSpec((box_dev, per_gen, lanes), lambda i, s: (0, 0, s[0] ^ k))

    with jax.named_scope("exchange_generators"):
        cot_rows = box_dev * per_gen * lanes // depth
        msgs = call(
            functools.partial(fold_kernel, size - 1),
            scalars,
            [gens] * ((size - 1) * HALVES) + [gens_cot] * (size - 1),
            [gens_spec(k, h) for h in halves for k in others] + [cot_spec(k) for k in others],
            [
                shape((group + (cot_rows if h == HALVES - 1 else 0), depth), BF)
                for h in halves
                for k in others
            ],
            cost(0, 1 << 20),
        )
        recv = [
            [over_gen(msgs[h * (size - 1) + k - 1], k) for k in others] for h in halves
        ]
    with jax.named_scope("swap_cores"):
        w_other = over_core(weight)
        stacked = jnp.stack([phase.astype(F32), center_cot, offset_cot])

        def small(core):
            part = lax.dynamic_slice_in_dim(stacked, core * core_boxes, core_boxes, 1)
            pad = jnp.zeros((8 - 3 * core_boxes - 1, cols), F32)
            return jnp.concatenate([part.reshape(3 * core_boxes, cols), bias[None], pad], 0)

        small_own = small(c)
        small_oth = over_core(small(1 - c))
    lefts, sums = [], []
    for h in halves:
        last = h == HALVES - 1
        with jax.named_scope("forward"):
            a_part, *res = call(
                functools.partial(forward_kernel, size, h),
                scalars,
                [gens, center, weight, w_other, *recv[h]] + [gens_cot] * last,
                [
                    gens_spec(0, h),
                    pl.BlockSpec((box_dev, depth), lambda i, s: (0, s[0])),
                    whole(weight),
                    whole(w_other),
                    *[whole(r) for r in recv[h]],
                ]
                + [cot_spec(0)] * last,
                [shape((work, depth), BF)]
                + [shape((HALVES * rows, lanes), BF)] * (2 * last)
                + [shape((rows + 8, 2 * lanes), F32)] * size,
                cost(2 * rows * depth * 2 * cols, 4 << 20),
            )
            if last:
                cot_keep, cot_send, *res = res
        lefts.append(a_part)
        with jax.named_scope("sum_products"):
            sums.append([res[0]] + [over_gen(res[k], k) for k in others])
    cot_got = over_core(cot_send)
    with jax.named_scope("share_generators"):
        a_own = jnp.concatenate(lefts, 0)
        a_core = over_core(a_own)
        a_box = over_box(a_own)
        a_box_core = over_core(a_box)
        pieces = [a_own, a_core, a_box, a_box_core]
        left = pl.pallas_call(
            stack_kernel,
            out_shape=shape((depth, 4 * HALVES * work), BF),
            compiler_params=params(),
            cost_estimate=cost(0, 5 << 20),
        )(*pieces)
    rights, finals = [[], [], [], []], []
    small_spec = pl.BlockSpec((8, lanes), lambda i, s: (0, s[0]))
    for h in halves:
        cot_part = pl.BlockSpec((rows, lanes), lambda i, s, h=h: (h, 0))
        with jax.named_scope("relax"):
            back, go, *msgs = call(
                functools.partial(relax_kernel, size, boxes, h),
                scalars,
                [*sums[h], cot_keep, cot_got, small_own, small_oth],
                [*[whole(p) for p in sums[h]], cot_part, cot_part, small_spec, small_spec],
                [
                    shape((work, 2 * lanes), BF),
                    shape((group, 2 * lanes), BF),
                    *[shape((work + group, 2 * lanes), BF)] * (size - 1),
                ],
                cost(rows * lanes * 20, 2 << 20),
                [pltpu.VMEM((rows, 2 * lanes), BF)],
            )
        with jax.named_scope("exchange_back"):
            got = [over_gen(m, k) for k, m in zip(others, msgs)]
            b_own, b_oth = call(
                spread_kernel,
                scalars,
                [back, go, *got],
                [whole(back), whole(go), *[whole(r) for r in got]],
                [shape((work + group, cols), BF)] * 2,
                cost(0, 2 << 20),
            )
            b_core = over_core(b_oth)
            b_box = over_box(b_own[:work])
            b_box_core = over_box(b_core[:work])
            for right, piece in zip(rights, (b_own, b_core, b_box, b_box_core)):
                right.append(piece)
        with jax.named_scope("input_gradient"):
            both = 2 * group + 8
            send, keep = call(
                functools.partial(input_grad_kernel, size),
                scalars,
                [b_own, b_oth, weight, w_other],
                [whole(b_own), whole(b_oth), whole(weight), whole(w_other)],
                [shape((both, depth), BF), shape((both, depth), F32)],
                cost(2 * rows * depth * 2 * cols, 4 << 20),
                [pltpu.VMEM((work, depth), F32)],
            )
            far = over_x(send)
            msgs = call(
                input_pair_kernel,
                scalars,
                [keep, far],
                [whole(keep), whole(far)],
                [shape((group + 8, depth), BF)] * 2,
                cost(0, 1 << 20),
                [pltpu.VMEM((both, depth), F32)],
            )
            finals += [turned(m, k) for k, m in enumerate(msgs)]
    with jax.named_scope("weight_gradient"):
        blocks = 4
        rights = [piece for right in rights for piece in right]
        out_shape = [
            shape((depth, cols), F32),
            shape((1, cols), F32),
            shape((box_dev, cols), F32),
            shape((box_dev, cols), F32),
            shape((box_dev, per_gen, cols), BF),
        ]
        weight_grad, bias_grad, center_out, offset, gens_out = pl.pallas_call(
            functools.partial(weight_grad_kernel, boxes),
            grid_spec=pltpu.PrefetchScalarGridSpec(
                num_scalar_prefetch=1,
                grid=(blocks,),
                in_specs=[pl.BlockSpec((depth // blocks, left.shape[1]), lambda i, s: (i, 0))]
                + [whole(r) for r in rights],
                out_specs=[pl.BlockSpec((depth // blocks, cols), lambda i, s: (i, 0))]
                + [whole(o) for o in out_shape[1:]],
                scratch_shapes=[pltpu.VMEM((left.shape[1], cols), BF)],
            ),
            out_shape=out_shape,
            compiler_params=params(),
            cost_estimate=cost(2 * left.shape[1] * depth * cols, 6 << 20),
        )(scalars, left, *rights)
    with jax.named_scope("input_gradient"):
        gens_grad, center_grad = call(
            functools.partial(input_final_kernel, boxes),
            scalars,
            [*finals, bias_grad],
            [*[whole(r) for r in finals], pl.BlockSpec(memory_space=pl.ANY)],
            [shape((box_dev, per_gen, depth), F32), shape((box_dev, depth), F32)],
            cost(0, 2 << 20),
        )
    return (
        center_out,
        gens_out,
        offset,
        weight_grad,
        bias_grad.reshape(cols),
        gens_grad,
        center_grad,
    )


def solution(mesh):
    sizes = dict(mesh.shape)

    def run(gens, center, weight, bias, phase, gens_cot, center_cot, offset_cot):
        size = sizes["gen"]
        box_dev = gens.shape[0] // sizes["box"]
        per_gen = gens.shape[1] // size
        cols = weight.shape[1] // sizes["neur"]
        square = (
            size == sizes["neur"] == 4
            and sizes["box"] == 2
            and box_dev == 4
            and per_gen % 16 == 0
            and cols % (128 * size) == 0
            and weight.shape[0] % (1024 * size) == 0
        )
        body = functools.partial(square_body, size) if square else general_body
        return jax.shard_map(
            body,
            mesh=mesh,
            in_specs=(
                P("box", "gen", None),
                P("box", None),
                P("gen", "neur"),
                P("neur"),
                P("box", "neur"),
                P("box", "gen", "neur"),
                P("box", "neur"),
                P("box", "neur"),
            ),
            out_specs=(
                P("box", "neur"),
                P("box", "gen", "neur"),
                P("box", "neur"),
                P("gen", "neur"),
                P("neur"),
                P("box", "gen", "neur"),
                P("box", "neur"),
            ),
            check_vma=False,
        )(gens, center, weight, bias, phase, gens_cot, center_cot, offset_cot)

    return run
```

```python
import functools

import jax
import jax.numpy as jnp
from jax import lax
from jax.experimental import pallas as pl
from jax.experimental.pallas import tpu as pltpu
from jax.sharding import PartitionSpec as P

BF = jnp.bfloat16
F32 = jnp.float32
VMEM_LIMIT = 24 * 1024 * 1024


def neuron(center_pre, radius, phase):
    upper = center_pre + radius
    lower = center_pre - radius
    ratio = jnp.clip(upper / (upper - lower + 1e-05), 0.0, 1.0)
    active = (phase == 1).astype(center_pre.dtype)
    crossing = (phase == 2).astype(center_pre.dtype)
    slope = active + crossing * ratio
    offset = crossing * (-ratio * lower * 0.5)
    return (slope, slope * center_pre + offset, offset)


def general_body(gens, center, weight, bias, phase, gens_cot, center_cot, offset_cot):
    box_dev, gen_dev, width = gens.shape
    local_cols = weight.shape[1]
    local_rows = box_dev * gen_dev
    wide = jnp.concatenate([gens.reshape(local_rows, width), center], 0)
    full_weight = lax.all_gather(weight, "gen", axis=0, tiled=True)
    product = jnp.dot(wide, full_weight, preferred_element_type=F32)
    gen_pre = product[:local_rows].reshape(box_dev, gen_dev, local_cols)
    center_pre = product[local_rows:] + bias
    part_radius = jnp.sum(jnp.abs(gen_pre), axis=1)
    cot_wide = gens_cot.astype(F32)
    radius = lax.psum(part_radius, "gen")
    slope, center_out, offset = neuron(center_pre, radius, phase)
    gens_out = (slope[:, None, :] * gen_pre).astype(BF)
    intersection = lax.psum(jnp.sum(cot_wide * gen_pre, axis=1), "gen")
    unused, pull = jax.vjp(lambda a, b: neuron(a, b, phase), center_pre, radius)
    g_center, g_radius = pull((intersection, center_cot, offset_cot))
    gen_back = (slope[:, None, :] * cot_wide + jnp.sign(gen_pre) * g_radius[:, None, :]).astype(BF)
    center_back = g_center.astype(BF)
    back = jnp.concatenate([gen_back.reshape(local_rows, local_cols), center_back], 0)
    first_gen = (lax.axis_index("gen") == 0).astype(BF)
    back_owned = jnp.concatenate(
        [gen_back.reshape(local_rows, local_cols), center_back * first_gen], 0
    )
    shares = lax.psum_scatter(
        lax.dot_general(wide, back_owned, (((0,), (0,)), ((), ())), preferred_element_type=F32),
        ("gen", "box"),
        scatter_dimension=0,
        tiled=True,
    )
    weight_grad = lax.all_gather(shares, "box", axis=0, tiled=True)
    bias_grad = lax.psum(jnp.sum(g_center, axis=0), "box")
    partial_back = lax.dot_general(
        back, full_weight, (((1,), (1,)), ((), ())), preferred_element_type=F32
    )
    summed = lax.psum_scatter(partial_back, "neur", scatter_dimension=1, tiled=True)
    gens_grad = summed[:local_rows].reshape(box_dev, gen_dev, summed.shape[1])
    center_grad = summed[local_rows:]
    return (center_out, gens_out, offset, weight_grad, bias_grad, gens_grad, center_grad)


CENTER_ROWS = 16
HALVES = 1
ORDER = (0, 2, 3, 1)


def params():
    return pltpu.CompilerParams(vmem_limit_bytes=VMEM_LIMIT)


def shape(dims, dtype):
    return jax.ShapeDtypeStruct(dims, dtype)


def whole(x):
    return pl.BlockSpec(x.shape, lambda i, s, r=len(x.shape): (0,) * r)


def call(kernel, scalars, args, specs, outs, scratch=(), after=(), cost=(0, 1 << 20)):
    skip = len(after)

    def body(s_ref, *refs):
        kernel(s_ref, *refs[skip:])

    return pl.pallas_call(
        body,
        grid_spec=pltpu.PrefetchScalarGridSpec(
            num_scalar_prefetch=1,
            grid=(1,),
            in_specs=[pl.BlockSpec(memory_space=pl.ANY)] * skip + specs,
            out_specs=[whole(o) for o in outs],
            scratch_shapes=list(scratch),
        ),
        out_shape=outs,
        compiler_params=params(),
        cost_estimate=pl.CostEstimate(flops=cost[0], bytes_accessed=cost[1], transcendentals=0),
    )(scalars, *after, *args)


def rows_at(index, size):
    return pl.ds(pl.multiple_of(index * size, size), size)


def fold_kernel(size, s_ref, gens_ref, cot_ref, *refs):
    g, c = s_ref[0], s_ref[1]
    outs, cot, sems = refs[:size], refs[-2], refs[-1]
    core_boxes, per_gen = gens_ref.shape[0] // 2, gens_ref.shape[1]
    depth = outs[0].shape[1]
    copies = [pltpu.make_async_copy(cot_ref, cot, sems.at[0])]
    for k, out in zip(ORDER, outs):
        for b in range(core_boxes):
            source = gens_ref.at[c * core_boxes + b, :, rows_at(g ^ k, depth)]
            target = out.at[pl.ds(b * per_gen, per_gen), :]
            copies.append(pltpu.make_async_copy(source, target, sems.at[len(copies)]))
    for copy in copies:
        copy.start()
    for copy in copies:
        copy.wait()
    rows, lanes = core_boxes * per_gen, cot.shape[2] // size
    for k, out in zip(ORDER, outs):
        value = cot[:, :, rows_at(g ^ k, lanes)].reshape(-1, lanes)
        per = out.shape[0] - rows
        for i in range(value.shape[0] // per):
            out[rows:, i * lanes : (i + 1) * lanes] = value[i * per : (i + 1) * per]


def copy_kernel(s_ref, in_ref, out_ref):
    out_ref[...] = in_ref[...]


def forward_kernel(size, s_ref, center_ref, own_ref, oth_ref, *refs):
    g, c = s_ref[0], s_ref[1]
    recv, (a_ref, keep_ref, send_ref), products = refs[:size], refs[size : size + 3], refs[size + 3 :]
    work, depth = a_ref.shape[0] // HALVES, a_ref.shape[1]
    group = (work - CENTER_ROWS) // size
    mid = center_ref[...].astype(F32)
    core_boxes = mid.shape[0] // 2
    boxes = core_boxes // HALVES
    mid = jnp.where(c == 0, mid[:core_boxes], mid[core_boxes:])
    pad = jnp.zeros((CENTER_ROWS - boxes, depth), F32)
    lanes = products[0].shape[1] // 2
    for h in range(HALVES):
        for k, msg in zip(ORDER, recv):
            at = pl.ds(pl.multiple_of(h * work + (g ^ k) * group, CENTER_ROWS), group)
            a_ref[at, :] = msg[h * group : (h + 1) * group, :]
        tail = jnp.concatenate([mid[h * boxes : (h + 1) * boxes], pad], 0).astype(BF)
        a_ref[(h + 1) * work - CENTER_ROWS : (h + 1) * work, :] = tail
    a = a_ref[...]
    for i, k in enumerate(ORDER):
        at = rows_at(g ^ k, lanes)
        w = jnp.concatenate([own_ref[:, at], oth_ref[:, at]], 1)
        product = jnp.dot(a, w, preferred_element_type=F32)
        for h in range(HALVES):
            out = products[h * size + i]
            out[...] = product[h * work : h * work + out.shape[0]]
    rows = HALVES * group
    for k, msg in zip(ORDER, recv):
        cot = [msg[rows:, i * lanes : (i + 1) * lanes] for i in range(depth // lanes)]
        cot = jnp.concatenate(cot, 0)
        low, high = cot[:rows], cot[rows:]
        for ref, value in (
            (keep_ref, jnp.where(c == 0, low, high)),
            (send_ref, jnp.where(c == 0, high, low)),
        ):
            for h in range(HALVES):
                at = pl.ds(pl.multiple_of(h * size * group + (g ^ k) * group, group), group)
                ref[at, :] = value[h * group : (h + 1) * group]


def relax_kernel(size, boxes, part, s_ref, *refs):
    g = s_ref[0]
    sums, (keep_ref, got_ref, own_ref, oth_ref), outs = refs[:size], refs[size : size + 4], refs[size + 4 :]
    back_ref, go_ref, msgs, out_scratch = outs[0], outs[1], outs[2:-1], outs[-1]
    pre = sums[0][...]
    for p in sums[1:]:
        pre = pre + p[...]
    group = go_ref.shape[0]
    rows, per = size * group, group // boxes
    cot = jnp.concatenate([keep_ref[...], got_ref[...]], 1).astype(F32)
    small = jnp.concatenate([own_ref[...], oth_ref[...]], 1)
    step = HALVES * boxes
    phase, center_cot, offset_cot = (
        small[i * step + part * boxes : i * step + (part + 1) * boxes] for i in range(3)
    )
    bias = small[3 * step : 3 * step + 1]
    where = [[q * group + b * per for q in range(size)] for b in range(boxes)]
    radius, cross = [], []
    for b in range(boxes):
        radius.append(sum(jnp.sum(jnp.abs(pre[r : r + per]), 0, keepdims=True) for r in where[b]))
        cross.append(sum(jnp.sum(cot[r : r + per] * pre[r : r + per], 0, keepdims=True) for r in where[b]))
    radius, cross = jnp.concatenate(radius, 0), jnp.concatenate(cross, 0)
    center_pre = pre[rows : rows + boxes] + bias
    (slope, center_out, offset), pull = jax.vjp(lambda a, b: neuron(a, b, phase), center_pre, radius)
    g_center, g_radius = pull((cross, center_cot, offset_cot))
    for b in range(boxes):
        sl, gr = slope[b : b + 1], g_radius[b : b + 1]
        for r in where[b]:
            x = pre[r : r + per]
            sign = jnp.where(x > 0, gr, jnp.where(x < 0, -gr, 0.0))
            back_ref[r : r + per, :] = (sl * cot[r : r + per] + sign).astype(BF)
            out_scratch[r : r + per, :] = (sl * x).astype(BF)
    tail = []
    for value in (g_center, center_out, offset):
        high = value.astype(BF).astype(F32)
        tail += [high, value - high]
    tail.append(jnp.zeros((CENTER_ROWS - 6 * boxes, value.shape[1]), F32))
    back_ref[rows:, :] = jnp.concatenate(tail, 0).astype(BF)
    go_ref[...] = out_scratch[rows_at(g, group), :]
    for k, msg in zip(ORDER[1:], msgs):
        msg[: rows + CENTER_ROWS, :] = back_ref[...]
        msg[rows + CENTER_ROWS :, :] = out_scratch[rows_at(g ^ k, group), :]


def spread_kernel(s_ref, back_ref, go_ref, *refs):
    g = s_ref[0]
    msgs, (full_ref, oth_ref, out_ref) = refs[:-3], refs[-3:]
    rows, lanes = back_ref.shape[0], back_ref.shape[1] // 2
    cols = oth_ref.shape[1]
    for i, k in enumerate(ORDER):
        at = rows_at(g ^ k, lanes)
        right = pl.ds(pl.multiple_of(cols + (g ^ k) * lanes, lanes), lanes)
        back, out = (back_ref, go_ref[...]) if i == 0 else (msgs[i - 1], msgs[i - 1][rows:, :])
        full_ref[:, at] = back[:rows, :lanes]
        full_ref[:, right] = back[:rows, lanes:]
        oth_ref[:rows, at] = back[:rows, lanes:]
        oth_ref[rows:, at] = out[:, lanes:]
        out_ref[:, at] = out[:, :lanes]


def input_grad_kernel(size, s_ref, full_ref, w_own_ref, w_oth_ref, *refs):
    c, x = s_ref[1], s_ref[2] >> 1
    outs, res = refs[:-1], refs[-1]
    rows, cols = res.shape[0], w_own_ref.shape[1]
    over = (((1,), (1,)), ((), ()))
    res[...] = lax.dot_general(
        full_ref[:, :cols], w_own_ref[...], over, preferred_element_type=F32
    ) + lax.dot_general(full_ref[:, cols:], w_oth_ref[...], over, preferred_element_type=F32)
    group = (rows - CENTER_ROWS) // size
    tail = res[size * group : size * group + 8, :]
    for i, ref in enumerate(outs):
        at = (1 - x if i < 2 else x) + 2 * (c ^ (i % 2))
        ref[...] = jnp.concatenate([res[rows_at(at, group), :], tail], 0).astype(ref.dtype)


def input_pair_kernel(s_ref, keep_ref, far_ref, out_ref):
    out_ref[...] = (keep_ref[...] + far_ref[...].astype(F32)).astype(BF)


def input_final_kernel(boxes, s_ref, *refs):
    msgs, (grad_ref, center_ref) = refs[:-2], refs[-2:]
    first = s_ref[0] >> 1
    per = grad_ref.shape[1]
    group = boxes * per
    rows = [[], []]
    for h in range(HALVES):
        for k in range(2):
            value = msgs[k][h * (group + 8) : (h + 1) * (group + 8), :].astype(F32)
            at = (first ^ k) * (HALVES * boxes) + h * boxes
            grad_ref[pl.ds(at, boxes)] = value[:group].reshape(boxes, per, -1)
            rows[k].append(value[group : group + boxes])
    near, far = (jnp.concatenate(r, 0) for r in rows)
    center_ref[...] = jnp.where(
        first == 0, jnp.concatenate([near, far], 0), jnp.concatenate([far, near], 0)
    )


def stack_kernel(s_ref, *refs):
    lefts, out = refs[:-1], refs[-1]
    rows = lefts[0].shape[0] // HALVES
    gens = rows - CENTER_ROWS
    tails = []
    for i in range(len(lefts) * HALVES):
        ref, h = lefts[i // HALVES], i % HALVES
        out[:, i * gens : (i + 1) * gens] = ref[h * rows : h * rows + gens, :].T
        tails.append(ref[h * rows + gens : (h + 1) * rows, :])
    width = out.shape[1] - len(lefts) * HALVES * gens
    pad = jnp.zeros((width - len(tails) * CENTER_ROWS, out.shape[0]), BF)
    out[:, len(tails) * gens :] = jnp.concatenate(tails + [pad], 0).T


def weight_grad_kernel(boxes, s_ref, after_ref, left_ref, *refs):
    rights, keeps, refs = refs[: 4 * HALVES], refs[4 * HALVES : 5 * HALVES], refs[5 * HALVES :]
    weight_ref, bias_ref, center_ref, offset_ref, gens_ref, done_ref, stack = refs
    per = gens_ref.shape[1]
    cols = weight_ref.shape[1]
    gens = rights[-1].shape[0] - CENTER_ROWS

    @pl.when(pl.program_id(0) == 0)
    def _():
        c = s_ref[1]
        done_ref[...] = jnp.zeros(done_ref.shape, F32)
        tails = []
        for i, right in enumerate(rights):
            stack[i * gens : (i + 1) * gens, :] = right[:gens, :cols]
            tail = right[gens : gens + CENTER_ROWS, :cols]
            at = len(rights) * gens + i * CENTER_ROWS
            stack[at : at + CENTER_ROWS, :] = tail
            tails.append(tail.astype(F32))
        used = len(rights) * (gens + CENTER_ROWS)
        if used < stack.shape[0]:
            stack[used:, :] = jnp.zeros((stack.shape[0] - used, cols), BF)
        bias_ref[...] = sum(jnp.sum(t[: 2 * boxes], 0, keepdims=True) for t in tails)
        for at, ref in ((2, center_ref), (4, offset_ref)):
            both = [
                t[at * boxes : (at + 1) * boxes] + t[(at + 1) * boxes : (at + 2) * boxes]
                for t in tails[: 2 * HALVES]
            ]
            mine, other = (jnp.concatenate(both[i * HALVES : (i + 1) * HALVES], 0) for i in range(2))
            ref[...] = jnp.where(
                c == 0, jnp.concatenate([mine, other], 0), jnp.concatenate([other, mine], 0)
            )
        for h in range(HALVES):
            for at, out in ((c, keeps[h][...]), (1 - c, rights[HALVES + h][gens + CENTER_ROWS :, :])):
                at = at * (HALVES * boxes) + h * boxes
                gens_ref[pl.ds(at, boxes)] = out.reshape(boxes, per, -1)

    weight_ref[...] = jnp.dot(left_ref[...], stack[...], preferred_element_type=F32)


def square_body(size, gens, center, weight, bias, phase, gens_cot, center_cot, offset_cot):
    box_dev, per_gen, width = gens.shape
    depth, cols = weight.shape
    core_boxes = box_dev // 2
    boxes = core_boxes // HALVES
    group = boxes * per_gen
    rows = size * group
    work = rows + CENTER_ROWS
    lanes = cols // size
    g, n = lax.axis_index("gen"), lax.axis_index("neur")
    c = n % 2
    scalars = jnp.stack([g, c, n, lax.axis_index("box")]).astype(jnp.int32)
    halves = range(HALVES)

    def over_gen(pieces):
        return [pieces[0]] + [
            lax.ppermute(piece, "gen", [(i, i ^ k) for i in range(size)])
            for piece, k in zip(pieces[1:], ORDER[1:])
        ]

    def over_core(x):
        return lax.ppermute(x, "neur", [(i, i ^ 1) for i in range(size)])

    def over_x(x):
        return lax.ppermute(x, "neur", [(i, i ^ 2) for i in range(size)])

    def over_box(x):
        return lax.ppermute(x, "box", [(0, 1), (1, 0)])

    def turned(x, k):
        pairs = [
            (i * size + j, ((j >> 1) + 2 * ((j & 1) ^ k)) * size + i)
            for i in range(size)
            for j in range(size)
        ]
        return lax.ppermute(x, ("gen", "neur"), pairs)

    anywhere = pl.BlockSpec(memory_space=pl.ANY)
    with jax.named_scope("exchange_generators"):
        cot_rows = box_dev * per_gen * lanes // depth
        msgs = call(
            functools.partial(fold_kernel, size),
            scalars,
            [gens, gens_cot],
            [anywhere] * 2,
            [shape((core_boxes * per_gen + cot_rows, depth), BF)] * size,
            [pltpu.VMEM(gens_cot.shape, BF), pltpu.SemaphoreType.DMA((size * core_boxes + 1,))],
            cost=(0, 32 << 20),
        )
        recv = over_gen(msgs)
    with jax.named_scope("swap_cores"):
        w_other = over_core(weight)
        (w_back,) = call(
            copy_kernel, scalars, [w_other], [whole(w_other)], [shape(weight.shape, BF)], after=msgs[:1]
        )
        w_own = over_core(w_back)
        center = over_core(center)
        stacked = jnp.stack([phase.astype(F32), center_cot, offset_cot])

        def small(core):
            part = lax.dynamic_slice_in_dim(stacked, core * core_boxes, core_boxes, 1)
            pad = jnp.zeros((8 - 3 * core_boxes - 1, cols), F32)
            return jnp.concatenate([part.reshape(3 * core_boxes, cols), bias[None], pad], 0)

        small_own = small(c)
        small_oth = over_core(small(1 - c))
    with jax.named_scope("forward"):
        a_own, cot_keep, cot_send, *products = call(
            functools.partial(forward_kernel, size),
            scalars,
            [center, w_own, w_other, *recv],
            [
                pl.BlockSpec((box_dev, depth), lambda i, s: (0, s[0])),
                whole(w_own),
                whole(w_other),
                *[whole(r) for r in recv],
            ],
            [shape((HALVES * work, depth), BF)]
            + [shape((HALVES * rows, lanes), BF)] * 2
            + [shape((rows + 8, 2 * lanes), F32)] * (HALVES * size),
            cost=(2 * HALVES * rows * depth * 2 * cols, 4 << 20),
        )
    with jax.named_scope("sum_products"):
        sums = []
        for h in halves:
            sums.append(over_gen(products[h * size : (h + 1) * size]))
        cot_got = over_core(cot_send)
    with jax.named_scope("share_generators"):
        a_box = over_box(a_own)
        pieces = [a_own, over_core(a_own), a_box, over_core(a_box)]
        (left,) = call(
            stack_kernel,
            scalars,
            pieces,
            [whole(v) for v in pieces],
            [shape((depth, 4 * HALVES * rows + 128), BF)],
        )
    keeps, sends = [], []
    small_spec = pl.BlockSpec((8, lanes), lambda i, s: (0, s[0]))
    for h in halves:
        cot_part = pl.BlockSpec((rows, lanes), lambda i, s, h=h: (h, 0))
        with jax.named_scope("relax"):
            back, go, *msgs = call(
                functools.partial(relax_kernel, size, boxes, h),
                scalars,
                [*sums[h], cot_keep, cot_got, small_own, small_oth],
                [*[whole(p) for p in sums[h]], cot_part, cot_part, small_spec, small_spec],
                [
                    shape((work, 2 * lanes), BF),
                    shape((group, 2 * lanes), BF),
                    *[shape((work + group, 2 * lanes), BF)] * (size - 1),
                ],
                [pltpu.VMEM((rows, 2 * lanes), BF)],
            )
        with jax.named_scope("exchange_back"):
            got = over_gen([None, *msgs])[1:]
            full, oth, out_own = call(
                spread_kernel,
                scalars,
                [back, go, *got],
                [whole(back), whole(go), *[whole(r) for r in got]],
                [
                    shape((work, 2 * cols), BF),
                    shape((work + group, cols), BF),
                    shape((group, cols), BF),
                ],
                after=sends[-1][:1] if h else [],
            )
            full_box = over_box(full)
            core_part = over_core(oth)
            keeps.append(out_own)
        with jax.named_scope("input_gradient"):
            both = group + 8
            sends.append(
                call(
                    functools.partial(input_grad_kernel, size),
                    scalars,
                    [full, w_own, w_other],
                    [whole(full), whole(w_own), whole(w_other)],
                    [shape((both, depth), BF)] * 2 + [shape((both, depth), F32)] * 2,
                    [pltpu.VMEM((work, depth), F32)],
                    cost=(2 * rows * depth * 2 * cols, 4 << 20),
                )
            )
    with jax.named_scope("input_gradient"):
        (send_0, send_1, *keeps_f32), = sends
        fars = [over_x(send_0), over_x(send_1)]
        pairs = []
        for keep, far in zip(keeps_f32, fars):
            pairs += call(
                input_pair_kernel,
                scalars,
                [keep, far],
                [whole(keep), whole(far)],
                [shape((group + 8, depth), BF)],
                after=pairs[-1:],
            )
        finals = [turned(m, k) for k, m in enumerate(pairs)]
        (box_oth,) = call(
            copy_kernel,
            scalars,
            [full_box],
            [pl.BlockSpec((work, cols), lambda i, s: (0, 1))],
            [shape((work, cols), BF)],
            after=pairs[-1:],
        )
        rights = [full, core_part, full_box, over_core(box_oth)]
    with jax.named_scope("weight_gradient"):
        blocks = 4
        out_shape = [
            shape((depth, cols), F32),
            shape((1, cols), F32),
            shape((box_dev, cols), F32),
            shape((box_dev, cols), F32),
            shape((box_dev, per_gen, cols), BF),
            shape((8, 128), F32),
        ]
        weight_grad, bias_grad, center_out, offset, gens_out, done = pl.pallas_call(
            functools.partial(weight_grad_kernel, boxes),
            grid_spec=pltpu.PrefetchScalarGridSpec(
                num_scalar_prefetch=1,
                grid=(blocks,),
                in_specs=[anywhere, pl.BlockSpec((depth // blocks, left.shape[1]), lambda i, s: (i, 0))]
                + [whole(r) for r in rights + keeps],
                out_specs=[pl.BlockSpec((depth // blocks, cols), lambda i, s: (i, 0))]
                + [whole(o) for o in out_shape[1:]],
                scratch_shapes=[pltpu.VMEM((left.shape[1], cols), BF)],
            ),
            out_shape=out_shape,
            compiler_params=params(),
            cost_estimate=pl.CostEstimate(
                flops=2 * left.shape[1] * depth * cols, bytes_accessed=6 << 20, transcendentals=0
            ),
        )(scalars, pairs[-1], left, *rights, *keeps)
    with jax.named_scope("input_gradient"):
        gens_grad, center_grad = call(
            functools.partial(input_final_kernel, boxes),
            scalars,
            finals,
            [whole(r) for r in finals],
            [shape((box_dev, per_gen, depth), F32), shape((box_dev, depth), F32)],
            after=[done],
        )
    return (
        center_out,
        gens_out,
        offset,
        weight_grad,
        bias_grad.reshape(cols),
        gens_grad,
        center_grad,
    )


def solution(mesh):
    sizes = dict(mesh.shape)

    def run(gens, center, weight, bias, phase, gens_cot, center_cot, offset_cot):
        size = sizes["gen"]
        box_dev = gens.shape[0] // sizes["box"]
        per_gen = gens.shape[1] // size
        cols = weight.shape[1] // sizes["neur"]
        square = (
            size == sizes["neur"] == 4
            and sizes["box"] == 2
            and box_dev == 4
            and per_gen % 16 == 0
            and cols % (128 * size) == 0
            and weight.shape[0] % (1024 * size) == 0
        )
        body = functools.partial(square_body, size) if square else general_body
        return jax.shard_map(
            body,
            mesh=mesh,
            in_specs=(
                P("box", "gen", None),
                P("box", None),
                P("gen", "neur"),
                P("neur"),
                P("box", "neur"),
                P("box", "gen", "neur"),
                P("box", "neur"),
                P("box", "neur"),
            ),
            out_specs=(
                P("box", "neur"),
                P("box", "gen", "neur"),
                P("box", "neur"),
                P("gen", "neur"),
                P("neur"),
                P("box", "gen", "neur"),
                P("box", "neur"),
            ),
            check_vma=False,
        )(gens, center, weight, bias, phase, gens_cot, center_cot, offset_cot)

    return run
```

```python
import functools

import jax
import jax.numpy as jnp
from jax import lax
from jax.experimental import pallas as pl
from jax.experimental.pallas import tpu as pltpu
from jax.sharding import PartitionSpec as P

BF = jnp.bfloat16
F32 = jnp.float32
VMEM_LIMIT = 32 * 1024 * 1024


def neuron(center_pre, radius, phase):
    upper = center_pre + radius
    lower = center_pre - radius
    ratio = jnp.clip(upper / (upper - lower + 1e-05), 0.0, 1.0)
    active = (phase == 1).astype(center_pre.dtype)
    crossing = (phase == 2).astype(center_pre.dtype)
    slope = active + crossing * ratio
    offset = crossing * (-ratio * lower * 0.5)
    return (slope, slope * center_pre + offset, offset)


def general_body(gens, center, weight, bias, phase, gens_cot, center_cot, offset_cot):
    box_dev, gen_dev, width = gens.shape
    local_cols = weight.shape[1]
    local_rows = box_dev * gen_dev
    wide = jnp.concatenate([gens.reshape(local_rows, width), center], 0)
    full_weight = lax.all_gather(weight, "gen", axis=0, tiled=True)
    product = jnp.dot(wide, full_weight, preferred_element_type=F32)
    gen_pre = product[:local_rows].reshape(box_dev, gen_dev, local_cols)
    center_pre = product[local_rows:] + bias
    part_radius = jnp.sum(jnp.abs(gen_pre), axis=1)
    cot_wide = gens_cot.astype(F32)
    radius = lax.psum(part_radius, "gen")
    slope, center_out, offset = neuron(center_pre, radius, phase)
    gens_out = (slope[:, None, :] * gen_pre).astype(BF)
    intersection = lax.psum(jnp.sum(cot_wide * gen_pre, axis=1), "gen")
    unused, pull = jax.vjp(lambda a, b: neuron(a, b, phase), center_pre, radius)
    g_center, g_radius = pull((intersection, center_cot, offset_cot))
    gen_back = (slope[:, None, :] * cot_wide + jnp.sign(gen_pre) * g_radius[:, None, :]).astype(BF)
    center_back = g_center.astype(BF)
    back = jnp.concatenate([gen_back.reshape(local_rows, local_cols), center_back], 0)
    first_gen = (lax.axis_index("gen") == 0).astype(BF)
    back_owned = jnp.concatenate(
        [gen_back.reshape(local_rows, local_cols), center_back * first_gen], 0
    )
    shares = lax.psum_scatter(
        lax.dot_general(wide, back_owned, (((0,), (0,)), ((), ())), preferred_element_type=F32),
        ("gen", "box"),
        scatter_dimension=0,
        tiled=True,
    )
    weight_grad = lax.all_gather(shares, "box", axis=0, tiled=True)
    bias_grad = lax.psum(jnp.sum(g_center, axis=0), "box")
    partial_back = lax.dot_general(
        back, full_weight, (((1,), (1,)), ((), ())), preferred_element_type=F32
    )
    summed = lax.psum_scatter(partial_back, "neur", scatter_dimension=1, tiled=True)
    gens_grad = summed[:local_rows].reshape(box_dev, gen_dev, summed.shape[1])
    center_grad = summed[local_rows:]
    return (center_out, gens_out, offset, weight_grad, bias_grad, gens_grad, center_grad)


CENTER_ROWS = 16
HALVES = 1
ORDER = (0, 3, 2, 1)


def params():
    return pltpu.CompilerParams(vmem_limit_bytes=VMEM_LIMIT)


def shape(dims, dtype):
    return jax.ShapeDtypeStruct(dims, dtype)


def whole(x):
    return pl.BlockSpec(x.shape, lambda i, s, r=len(x.shape): (0,) * r)


def call(kernel, scalars, args, specs, outs, scratch=(), after=(), cost=None):
    skip = len(after)

    def body(s_ref, *refs):
        kernel(s_ref, *refs[skip:])

    return pl.pallas_call(
        body,
        grid_spec=pltpu.PrefetchScalarGridSpec(
            num_scalar_prefetch=1,
            grid=(1,),
            in_specs=[pl.BlockSpec(memory_space=pl.ANY)] * skip + specs,
            out_specs=[whole(o) for o in outs],
            scratch_shapes=list(scratch),
        ),
        out_shape=outs,
        compiler_params=params(),
        cost_estimate=cost and pl.CostEstimate(flops=cost[0], bytes_accessed=cost[1], transcendentals=0),
    )(scalars, *after, *args)


def rows_at(index, size):
    return pl.ds(pl.multiple_of(index * size, size), size)


def fold_kernel(size, s_ref, gens_ref, cot_ref, *refs):
    g, c = s_ref[0], s_ref[1]
    outs, cot, sems = refs[:size], refs[-2], refs[-1]
    core_boxes, per_gen = gens_ref.shape[0] // 2, gens_ref.shape[1]
    depth = outs[0].shape[1]
    copies = [pltpu.make_async_copy(cot_ref, cot, sems.at[0])]
    for k, out in zip(ORDER, outs):
        for b in range(core_boxes):
            source = gens_ref.at[c * core_boxes + b, :, rows_at(g ^ k, depth)]
            target = out.at[pl.ds(b * per_gen, per_gen), :]
            copies.append(pltpu.make_async_copy(source, target, sems.at[len(copies)]))
    for copy in copies:
        copy.start()
    for copy in copies:
        copy.wait()
    rows, lanes = core_boxes * per_gen, cot.shape[2] // size
    for k, out in zip(ORDER, outs):
        value = cot[:, :, rows_at(g ^ k, lanes)].reshape(-1, lanes)
        per = out.shape[0] - rows
        for i in range(value.shape[0] // per):
            out[rows:, i * lanes : (i + 1) * lanes] = value[i * per : (i + 1) * per]


def copy_kernel(s_ref, in_ref, out_ref):
    out_ref[...] = in_ref[...]


def forward_kernel(size, s_ref, center_ref, own_ref, oth_ref, *refs):
    g, c = s_ref[0], s_ref[1]
    recv, (a_ref, keep_ref, send_ref), products = refs[:size], refs[size : size + 3], refs[size + 3 :]
    work, depth = a_ref.shape[0] // HALVES, a_ref.shape[1]
    group = (work - CENTER_ROWS) // size
    mid = center_ref[...].astype(F32)
    core_boxes = mid.shape[0] // 2
    boxes = core_boxes // HALVES
    mid = jnp.where(c == 0, mid[:core_boxes], mid[core_boxes:])
    pad = jnp.zeros((CENTER_ROWS - boxes, depth), F32)
    lanes = products[0].shape[1] // 2
    for h in range(HALVES):
        for k, msg in zip(ORDER, recv):
            at = pl.ds(pl.multiple_of(h * work + (g ^ k) * group, CENTER_ROWS), group)
            a_ref[at, :] = msg[h * group : (h + 1) * group, :]
        tail = jnp.concatenate([mid[h * boxes : (h + 1) * boxes], pad], 0).astype(BF)
        a_ref[(h + 1) * work - CENTER_ROWS : (h + 1) * work, :] = tail
    a = a_ref[...]
    for i, k in enumerate(ORDER):
        at = rows_at(g ^ k, lanes)
        w = jnp.concatenate([own_ref[:, at], oth_ref[:, at]], 1)
        product = jnp.dot(a, w, preferred_element_type=F32)
        for h in range(HALVES):
            out = products[h * size + i]
            out[...] = product[h * work : h * work + out.shape[0]]
    rows = HALVES * group
    for k, msg in zip(ORDER, recv):
        cot = [msg[rows:, i * lanes : (i + 1) * lanes] for i in range(depth // lanes)]
        cot = jnp.concatenate(cot, 0)
        low, high = cot[:rows], cot[rows:]
        for ref, value in (
            (keep_ref, jnp.where(c == 0, low, high)),
            (send_ref, jnp.where(c == 0, high, low)),
        ):
            for h in range(HALVES):
                at = pl.ds(pl.multiple_of(h * size * group + (g ^ k) * group, group), group)
                ref[at, :] = value[h * group : (h + 1) * group]


def relax_kernel(size, boxes, part, s_ref, *refs):
    g = s_ref[0]
    sums, (keep_ref, got_ref, own_ref, oth_ref), outs = refs[:size], refs[size : size + 4], refs[size + 4 :]
    back_ref, go_ref, msgs, out_scratch = outs[0], outs[1], outs[2:-1], outs[-1]
    pre = sums[0][...]
    for p in sums[1:]:
        pre = pre + p[...]
    group = go_ref.shape[0]
    rows, per = size * group, group // boxes
    cot = jnp.concatenate([keep_ref[...], got_ref[...]], 1).astype(F32)
    small = jnp.concatenate([own_ref[...], oth_ref[...]], 1)
    step = HALVES * boxes
    phase, center_cot, offset_cot = (
        small[i * step + part * boxes : i * step + (part + 1) * boxes] for i in range(3)
    )
    bias = small[3 * step : 3 * step + 1]
    where = [[q * group + b * per for q in range(size)] for b in range(boxes)]
    radius, cross = [], []
    for b in range(boxes):
        radius.append(sum(jnp.sum(jnp.abs(pre[r : r + per]), 0, keepdims=True) for r in where[b]))
        cross.append(sum(jnp.sum(cot[r : r + per] * pre[r : r + per], 0, keepdims=True) for r in where[b]))
    radius, cross = jnp.concatenate(radius, 0), jnp.concatenate(cross, 0)
    center_pre = pre[rows : rows + boxes] + bias
    (slope, center_out, offset), pull = jax.vjp(lambda a, b: neuron(a, b, phase), center_pre, radius)
    g_center, g_radius = pull((cross, center_cot, offset_cot))
    for b in range(boxes):
        sl, gr = slope[b : b + 1], g_radius[b : b + 1]
        for r in where[b]:
            x = pre[r : r + per]
            sign = jnp.where(x > 0, gr, jnp.where(x < 0, -gr, 0.0))
            back_ref[r : r + per, :] = (sl * cot[r : r + per] + sign).astype(BF)
            out_scratch[r : r + per, :] = (sl * x).astype(BF)
    tail = []
    for value in (g_center, center_out, offset):
        high = value.astype(BF).astype(F32)
        tail += [high, value - high]
    tail.append(jnp.zeros((CENTER_ROWS - 6 * boxes, value.shape[1]), F32))
    back_ref[rows:, :] = jnp.concatenate(tail, 0).astype(BF)
    go_ref[...] = out_scratch[rows_at(g, group), :]
    for k, msg in zip(ORDER[1:], msgs):
        msg[: rows + CENTER_ROWS, :] = back_ref[...]
        msg[rows + CENTER_ROWS :, :] = out_scratch[rows_at(g ^ k, group), :]


def spread_kernel(s_ref, back_ref, go_ref, *refs):
    g = s_ref[0]
    msgs, (full_ref, oth_ref, out_ref) = refs[:-3], refs[-3:]
    rows, lanes = back_ref.shape[0], back_ref.shape[1] // 2
    cols = oth_ref.shape[1]
    for i, k in enumerate(ORDER):
        at = rows_at(g ^ k, lanes)
        right = pl.ds(pl.multiple_of(cols + (g ^ k) * lanes, lanes), lanes)
        back, out = (back_ref, go_ref[...]) if i == 0 else (msgs[i - 1], msgs[i - 1][rows:, :])
        full_ref[:, at] = back[:rows, :lanes]
        full_ref[:, right] = back[:rows, lanes:]
        oth_ref[:rows, at] = back[:rows, lanes:]
        oth_ref[rows:, at] = out[:, lanes:]
        out_ref[:, at] = out[:, :lanes]


def input_grad_kernel(size, s_ref, full_ref, w_own_ref, w_oth_ref, *refs):
    c, x = s_ref[1], s_ref[2] >> 1
    outs, res = refs[:-1], refs[-1]
    rows, cols = res.shape[0], w_own_ref.shape[1]
    over = (((1,), (1,)), ((), ()))
    res[...] = lax.dot_general(
        full_ref[:, :cols], w_own_ref[...], over, preferred_element_type=F32
    ) + lax.dot_general(full_ref[:, cols:], w_oth_ref[...], over, preferred_element_type=F32)
    group = (rows - CENTER_ROWS) // size
    tail = res[size * group : size * group + 8, :]
    for i, ref in enumerate(outs):
        at = (1 - x if i < 2 else x) + 2 * (c ^ (i % 2))
        ref[...] = jnp.concatenate([res[rows_at(at, group), :], tail], 0).astype(ref.dtype)


def input_pair_kernel(s_ref, keep_ref, far_ref, out_ref):
    out_ref[...] = (keep_ref[...] + far_ref[...].astype(F32)).astype(BF)


def input_final_kernel(boxes, s_ref, *refs):
    msgs, (grad_ref, center_ref) = refs[:-2], refs[-2:]
    first = s_ref[0] >> 1
    per = grad_ref.shape[1]
    group = boxes * per
    rows = [[], []]
    for h in range(HALVES):
        for k in range(2):
            value = msgs[k][h * (group + 8) : (h + 1) * (group + 8), :].astype(F32)
            at = (first ^ k) * (HALVES * boxes) + h * boxes
            grad_ref[pl.ds(at, boxes)] = value[:group].reshape(boxes, per, -1)
            rows[k].append(value[group : group + boxes])
    near, far = (jnp.concatenate(r, 0) for r in rows)
    center_ref[...] = jnp.where(
        first == 0, jnp.concatenate([near, far], 0), jnp.concatenate([far, near], 0)
    )


def stack_kernel(s_ref, *refs):
    lefts, out = refs[:-1], refs[-1]
    rows = lefts[0].shape[0] // HALVES
    gens = rows - CENTER_ROWS
    tails = []
    for i in range(len(lefts) * HALVES):
        ref, h = lefts[i // HALVES], i % HALVES
        out[:, i * gens : (i + 1) * gens] = ref[h * rows : h * rows + gens, :].T
        tails.append(ref[h * rows + gens : (h + 1) * rows, :])
    width = out.shape[1] - len(lefts) * HALVES * gens
    pad = jnp.zeros((width - len(tails) * CENTER_ROWS, out.shape[0]), BF)
    out[:, len(tails) * gens :] = jnp.concatenate(tails + [pad], 0).T


def weight_grad_kernel(boxes, s_ref, after_ref, left_ref, *refs):
    rights, keeps, refs = refs[: 4 * HALVES], refs[4 * HALVES : 5 * HALVES], refs[5 * HALVES :]
    weight_ref, bias_ref, center_ref, offset_ref, gens_ref, done_ref, stack = refs
    per = gens_ref.shape[1]
    cols = weight_ref.shape[1]
    gens = rights[-1].shape[0] - CENTER_ROWS

    @pl.when(pl.program_id(0) == 0)
    def _():
        c = s_ref[1]
        done_ref[...] = jnp.zeros(done_ref.shape, F32)
        tails = []
        for i, right in enumerate(rights):
            stack[i * gens : (i + 1) * gens, :] = right[:gens, :cols]
            tail = right[gens : gens + CENTER_ROWS, :cols]
            at = len(rights) * gens + i * CENTER_ROWS
            stack[at : at + CENTER_ROWS, :] = tail
            tails.append(tail.astype(F32))
        used = len(rights) * (gens + CENTER_ROWS)
        if used < stack.shape[0]:
            stack[used:, :] = jnp.zeros((stack.shape[0] - used, cols), BF)
        bias_ref[...] = sum(jnp.sum(t[: 2 * boxes], 0, keepdims=True) for t in tails)
        for at, ref in ((2, center_ref), (4, offset_ref)):
            both = [
                t[at * boxes : (at + 1) * boxes] + t[(at + 1) * boxes : (at + 2) * boxes]
                for t in tails[: 2 * HALVES]
            ]
            mine, other = (jnp.concatenate(both[i * HALVES : (i + 1) * HALVES], 0) for i in range(2))
            ref[...] = jnp.where(
                c == 0, jnp.concatenate([mine, other], 0), jnp.concatenate([other, mine], 0)
            )
        for h in range(HALVES):
            for at, out in ((c, keeps[h][...]), (1 - c, rights[HALVES + h][gens + CENTER_ROWS :, :])):
                at = at * (HALVES * boxes) + h * boxes
                gens_ref[pl.ds(at, boxes)] = out.reshape(boxes, per, -1)

    weight_ref[...] = jnp.dot(left_ref[...], stack[...], preferred_element_type=F32)


def square_body(size, gens, center, weight, bias, phase, gens_cot, center_cot, offset_cot):
    box_dev, per_gen, width = gens.shape
    depth, cols = weight.shape
    core_boxes = box_dev // 2
    boxes = core_boxes // HALVES
    group = boxes * per_gen
    rows = size * group
    work = rows + CENTER_ROWS
    lanes = cols // size
    g, n = lax.axis_index("gen"), lax.axis_index("neur")
    c = n % 2
    scalars = jnp.stack([g, c, n, lax.axis_index("box")]).astype(jnp.int32)
    halves = range(HALVES)

    def over_gen(pieces):
        return [pieces[0]] + [
            lax.ppermute(piece, "gen", [(i, i ^ k) for i in range(size)])
            for piece, k in zip(pieces[1:], ORDER[1:])
        ]

    def over_core(x):
        return lax.ppermute(x, "neur", [(i, i ^ 1) for i in range(size)])

    def over_x(x):
        return lax.ppermute(x, "neur", [(i, i ^ 2) for i in range(size)])

    def over_box(x):
        return lax.ppermute(x, "box", [(0, 1), (1, 0)])

    def turned(x, k):
        pairs = [
            (i * size + j, ((j >> 1) + 2 * ((j & 1) ^ k)) * size + i)
            for i in range(size)
            for j in range(size)
        ]
        return lax.ppermute(x, ("gen", "neur"), pairs)

    anywhere = pl.BlockSpec(memory_space=pl.ANY)
    with jax.named_scope("exchange_generators"):
        cot_rows = box_dev * per_gen * lanes // depth
        msgs = call(
            functools.partial(fold_kernel, size),
            scalars,
            [gens, gens_cot],
            [anywhere] * 2,
            [shape((core_boxes * per_gen + cot_rows, depth), BF)] * size,
            [pltpu.VMEM(gens_cot.shape, BF), pltpu.SemaphoreType.DMA((size * core_boxes + 1,))],
            cost=(0, 32 << 20),
        )
        recv = over_gen(msgs)
    with jax.named_scope("swap_cores"):
        w_other = over_core(weight)
        (w_near,) = call(
            copy_kernel, scalars, [weight], [whole(weight)], [shape(weight.shape, BF)], after=[recv[1]]
        )
        stacked = jnp.stack([phase.astype(F32), center_cot, offset_cot])

        def small(core):
            part = lax.dynamic_slice_in_dim(stacked, core * core_boxes, core_boxes, 1)
            pad = jnp.zeros((8 - 3 * core_boxes - 1, cols), F32)
            return jnp.concatenate([part.reshape(3 * core_boxes, cols), bias[None], pad], 0)

        small_own = small(c)
        small_oth = over_core(small(1 - c))
    with jax.named_scope("forward"):
        a_own, cot_keep, cot_send, *products = call(
            functools.partial(forward_kernel, size),
            scalars,
            [center, w_near, w_other, *recv],
            [
                pl.BlockSpec((box_dev, depth), lambda i, s: (0, s[0])),
                whole(w_near),
                whole(w_other),
                *[whole(r) for r in recv],
            ],
            [shape((HALVES * work, depth), BF)]
            + [shape((HALVES * rows, lanes), BF)] * 2
            + [shape((rows + 8, 2 * lanes), F32)] * (HALVES * size),
            cost=(2 * HALVES * rows * depth * 2 * cols, 4 << 20),
        )
    with jax.named_scope("sum_products"):
        sums = []
        for h in halves:
            sums.append(over_gen(products[h * size : (h + 1) * size]))
        cot_got = over_core(cot_send)
    with jax.named_scope("share_generators"):
        a_box = over_box(a_own)
        pieces = [a_own, over_core(a_own), a_box, over_core(a_box)]
        (left,) = call(
            stack_kernel,
            scalars,
            pieces,
            [whole(v) for v in pieces],
            [shape((depth, 4 * HALVES * rows + 128), BF)],
        )
    keeps, sends = [], []
    small_spec = pl.BlockSpec((8, lanes), lambda i, s: (0, s[0]))
    for h in halves:
        cot_part = pl.BlockSpec((rows, lanes), lambda i, s, h=h: (h, 0))
        with jax.named_scope("relax"):
            back, go, *msgs = call(
                functools.partial(relax_kernel, size, boxes, h),
                scalars,
                [*sums[h], cot_keep, cot_got, small_own, small_oth],
                [*[whole(p) for p in sums[h]], cot_part, cot_part, small_spec, small_spec],
                [
                    shape((work, 2 * lanes), BF),
                    shape((group, 2 * lanes), BF),
                    *[shape((work + group, 2 * lanes), BF)] * (size - 1),
                ],
                [pltpu.VMEM((rows, 2 * lanes), BF)],
            )
        with jax.named_scope("exchange_back"):
            got = over_gen([None, *msgs])[1:]
            full, oth, out_own = call(
                spread_kernel,
                scalars,
                [back, go, *got],
                [whole(back), whole(go), *[whole(r) for r in got]],
                [
                    shape((work, 2 * cols), BF),
                    shape((work + group, cols), BF),
                    shape((group, cols), BF),
                ],
            )
            core_part = over_core(oth)
            keeps.append(out_own)
        with jax.named_scope("input_gradient"):
            both = group + 8
            sends.append(
                call(
                    functools.partial(input_grad_kernel, size),
                    scalars,
                    [full, w_near, w_other],
                    [whole(full), whole(w_near), whole(w_other)],
                    [shape((both, depth), BF)] * 2 + [shape((both, depth), F32)] * 2,
                    [pltpu.VMEM((work, depth), F32)],
                    cost=(2 * rows * depth * 2 * cols, 4 << 20),
                )
            )
    with jax.named_scope("input_gradient"):
        (send_0, send_1, *keeps_f32), = sends
        def pair(keep, far, *after):
            (out,) = call(
                input_pair_kernel,
                scalars,
                [keep, far],
                [whole(keep), whole(far)],
                [shape((group + 8, depth), BF)],
                after=after,
            )
            return out

        first = pair(keeps_f32[0], over_x(send_0))
        full_box = over_box(full)
        finals = [turned(first, 0)]
        far_1 = over_x(send_1)
        last = pair(keeps_f32[1], far_1, finals[0])
        finals.append(turned(last, 1))
        (box_oth,) = call(
            copy_kernel,
            scalars,
            [full_box],
            [pl.BlockSpec((work, cols), lambda i, s: (0, 1))],
            [shape((work, cols), BF)],
            after=[last],
        )
        rights = [full, core_part, full_box, over_core(box_oth)]
    with jax.named_scope("weight_gradient"):
        blocks = 4
        out_shape = [
            shape((depth, cols), F32),
            shape((1, cols), F32),
            shape((box_dev, cols), F32),
            shape((box_dev, cols), F32),
            shape((box_dev, per_gen, cols), BF),
            shape((8, 128), F32),
        ]
        weight_grad, bias_grad, center_out, offset, gens_out, done = pl.pallas_call(
            functools.partial(weight_grad_kernel, boxes),
            grid_spec=pltpu.PrefetchScalarGridSpec(
                num_scalar_prefetch=1,
                grid=(blocks,),
                in_specs=[anywhere, pl.BlockSpec((depth // blocks, left.shape[1]), lambda i, s: (i, 0))]
                + [whole(r) for r in rights + keeps],
                out_specs=[pl.BlockSpec((depth // blocks, cols), lambda i, s: (i, 0))]
                + [whole(o) for o in out_shape[1:]],
                scratch_shapes=[pltpu.VMEM((left.shape[1], cols), BF)],
            ),
            out_shape=out_shape,
            compiler_params=params(),
        )(scalars, last, left, *rights, *keeps)
    with jax.named_scope("input_gradient"):
        gens_grad, center_grad = call(
            functools.partial(input_final_kernel, boxes),
            scalars,
            finals,
            [whole(r) for r in finals],
            [shape((box_dev, per_gen, depth), F32), shape((box_dev, depth), F32)],
            after=[done],
        )
    return (
        center_out,
        gens_out,
        offset,
        weight_grad,
        bias_grad.reshape(cols),
        gens_grad,
        center_grad,
    )


def solution(mesh):
    sizes = dict(mesh.shape)

    def run(gens, center, weight, bias, phase, gens_cot, center_cot, offset_cot):
        size = sizes["gen"]
        box_dev = gens.shape[0] // sizes["box"]
        per_gen = gens.shape[1] // size
        cols = weight.shape[1] // sizes["neur"]
        square = (
            size == sizes["neur"] == 4
            and sizes["box"] == 2
            and box_dev == 4
            and per_gen % 16 == 0
            and cols % (128 * size) == 0
            and weight.shape[0] % (1024 * size) == 0
        )
        body = functools.partial(square_body, size) if square else general_body
        return jax.shard_map(
            body,
            mesh=mesh,
            in_specs=(
                P("box", "gen", None),
                P("box", None),
                P("gen", "neur"),
                P("neur"),
                P("box", "neur"),
                P("box", "gen", "neur"),
                P("box", "neur"),
                P("box", "neur"),
            ),
            out_specs=(
                P("box", "neur"),
                P("box", "gen", "neur"),
                P("box", "neur"),
                P("gen", "neur"),
                P("neur"),
                P("box", "gen", "neur"),
                P("box", "neur"),
            ),
            check_vma=False,
        )(gens, center, weight, bias, phase, gens_cot, center_cot, offset_cot)

    return run
```

```python
import functools

import jax
import jax.numpy as jnp
from jax import lax
from jax.experimental import pallas as pl
from jax.experimental.pallas import tpu as pltpu
from jax.sharding import PartitionSpec as P

BF = jnp.bfloat16
F32 = jnp.float32
VMEM_LIMIT = 32 * 1024 * 1024


def neuron(center_pre, radius, phase):
    upper = center_pre + radius
    lower = center_pre - radius
    ratio = jnp.clip(upper / (upper - lower + 1e-05), 0.0, 1.0)
    active = (phase == 1).astype(center_pre.dtype)
    crossing = (phase == 2).astype(center_pre.dtype)
    slope = active + crossing * ratio
    offset = crossing * (-ratio * lower * 0.5)
    return (slope, slope * center_pre + offset, offset)


def general_body(gens, center, weight, bias, phase, gens_cot, center_cot, offset_cot):
    box_dev, gen_dev, width = gens.shape
    local_cols = weight.shape[1]
    local_rows = box_dev * gen_dev
    wide = jnp.concatenate([gens.reshape(local_rows, width), center], 0)
    full_weight = lax.all_gather(weight, "gen", axis=0, tiled=True)
    product = jnp.dot(wide, full_weight, preferred_element_type=F32)
    gen_pre = product[:local_rows].reshape(box_dev, gen_dev, local_cols)
    center_pre = product[local_rows:] + bias
    part_radius = jnp.sum(jnp.abs(gen_pre), axis=1)
    cot_wide = gens_cot.astype(F32)
    radius = lax.psum(part_radius, "gen")
    slope, center_out, offset = neuron(center_pre, radius, phase)
    gens_out = (slope[:, None, :] * gen_pre).astype(BF)
    intersection = lax.psum(jnp.sum(cot_wide * gen_pre, axis=1), "gen")
    unused, pull = jax.vjp(lambda a, b: neuron(a, b, phase), center_pre, radius)
    g_center, g_radius = pull((intersection, center_cot, offset_cot))
    gen_back = (slope[:, None, :] * cot_wide + jnp.sign(gen_pre) * g_radius[:, None, :]).astype(BF)
    center_back = g_center.astype(BF)
    back = jnp.concatenate([gen_back.reshape(local_rows, local_cols), center_back], 0)
    first_gen = (lax.axis_index("gen") == 0).astype(BF)
    back_owned = jnp.concatenate(
        [gen_back.reshape(local_rows, local_cols), center_back * first_gen], 0
    )
    shares = lax.psum_scatter(
        lax.dot_general(wide, back_owned, (((0,), (0,)), ((), ())), preferred_element_type=F32),
        ("gen", "box"),
        scatter_dimension=0,
        tiled=True,
    )
    weight_grad = lax.all_gather(shares, "box", axis=0, tiled=True)
    bias_grad = lax.psum(jnp.sum(g_center, axis=0), "box")
    partial_back = lax.dot_general(
        back, full_weight, (((1,), (1,)), ((), ())), preferred_element_type=F32
    )
    summed = lax.psum_scatter(partial_back, "neur", scatter_dimension=1, tiled=True)
    gens_grad = summed[:local_rows].reshape(box_dev, gen_dev, summed.shape[1])
    center_grad = summed[local_rows:]
    return (center_out, gens_out, offset, weight_grad, bias_grad, gens_grad, center_grad)


CENTER_ROWS = 16
HALVES = 1
ORDER = (0, 3, 2, 1)
COSTS = {"fold": 1000000, "copy": 1000000000, "forward": 1000000000, "relax": 1000000000}


def params():
    return pltpu.CompilerParams(vmem_limit_bytes=VMEM_LIMIT)


def shape(dims, dtype):
    return jax.ShapeDtypeStruct(dims, dtype)


def whole(x):
    return pl.BlockSpec(x.shape, lambda i, s, r=len(x.shape): (0,) * r)


def call(kernel, scalars, args, specs, outs, scratch=(), after=()):
    skip = len(after)
    cost = COSTS.get(getattr(kernel, "func", kernel).__name__.replace("_kernel", ""))

    def body(s_ref, *refs):
        kernel(s_ref, *refs[skip:])

    return pl.pallas_call(
        body,
        grid_spec=pltpu.PrefetchScalarGridSpec(
            num_scalar_prefetch=1,
            grid=(1,),
            in_specs=[pl.BlockSpec(memory_space=pl.ANY)] * skip + specs,
            out_specs=[whole(o) for o in outs],
            scratch_shapes=list(scratch),
        ),
        out_shape=outs,
        compiler_params=params(),
        cost_estimate=pl.CostEstimate(flops=cost, bytes_accessed=1 << 20, transcendentals=0) if cost else None,
    )(scalars, *after, *args)


def rows_at(index, size):
    return pl.ds(pl.multiple_of(index * size, size), size)


def fold_kernel(size, s_ref, gens_ref, cot_ref, *refs):
    g, c = s_ref[0], s_ref[1]
    outs, cot, sems = refs[:size], refs[-2], refs[-1]
    core_boxes, per_gen = gens_ref.shape[0] // 2, gens_ref.shape[1]
    depth = outs[0].shape[1]
    copies = [pltpu.make_async_copy(cot_ref, cot, sems.at[0])]
    for k, out in zip(ORDER, outs):
        for b in range(core_boxes):
            source = gens_ref.at[c * core_boxes + b, :, rows_at(g ^ k, depth)]
            target = out.at[pl.ds(b * per_gen, per_gen), :]
            copies.append(pltpu.make_async_copy(source, target, sems.at[len(copies)]))
    for copy in copies:
        copy.start()
    for copy in copies:
        copy.wait()
    rows, lanes = core_boxes * per_gen, cot.shape[2] // size
    for k, out in zip(ORDER, outs):
        value = cot[:, :, rows_at(g ^ k, lanes)].reshape(-1, lanes)
        per = out.shape[0] - rows
        for i in range(value.shape[0] // per):
            out[rows:, i * lanes : (i + 1) * lanes] = value[i * per : (i + 1) * per]


def chunk_kernel(s_ref, own_ref, oth_ref, out_ref):
    lanes = out_ref.shape[2] // 2
    for j in range(out_ref.shape[0]):
        out_ref[j, :, :lanes] = own_ref[:, j * lanes : (j + 1) * lanes]
        out_ref[j, :, lanes:] = oth_ref[:, j * lanes : (j + 1) * lanes]


def copy_kernel(s_ref, in_ref, out_ref):
    out_ref[...] = in_ref[...]


def forward_kernel(size, s_ref, center_ref, w_ref, *refs):
    g, c = s_ref[0], s_ref[1]
    recv, (a_ref, keep_ref, send_ref), products = refs[:size], refs[size : size + 3], refs[size + 3 :]
    work, depth = a_ref.shape[0] // HALVES, a_ref.shape[1]
    group = (work - CENTER_ROWS) // size
    mid = center_ref[...].astype(F32)
    core_boxes = mid.shape[0] // 2
    boxes = core_boxes // HALVES
    mid = jnp.where(c == 0, mid[:core_boxes], mid[core_boxes:])
    pad = jnp.zeros((CENTER_ROWS - boxes, depth), F32)
    lanes = products[0].shape[1] // 2
    for h in range(HALVES):
        for k, msg in zip(ORDER, recv):
            at = pl.ds(pl.multiple_of(h * work + (g ^ k) * group, CENTER_ROWS), group)
            a_ref[at, :] = msg[h * group : (h + 1) * group, :]
        tail = jnp.concatenate([mid[h * boxes : (h + 1) * boxes], pad], 0).astype(BF)
        a_ref[(h + 1) * work - CENTER_ROWS : (h + 1) * work, :] = tail
    a = a_ref[...]
    for i, k in enumerate(ORDER):
        product = jnp.dot(a, w_ref[g ^ k], preferred_element_type=F32)
        for h in range(HALVES):
            out = products[h * size + i]
            out[...] = product[h * work : h * work + out.shape[0]]
    rows = HALVES * group
    for k, msg in zip(ORDER, recv):
        cot = [msg[rows:, i * lanes : (i + 1) * lanes] for i in range(depth // lanes)]
        cot = jnp.concatenate(cot, 0)
        low, high = cot[:rows], cot[rows:]
        for ref, value in (
            (keep_ref, jnp.where(c == 0, low, high)),
            (send_ref, jnp.where(c == 0, high, low)),
        ):
            for h in range(HALVES):
                at = pl.ds(pl.multiple_of(h * size * group + (g ^ k) * group, group), group)
                ref[at, :] = value[h * group : (h + 1) * group]


def relax_kernel(size, boxes, part, s_ref, *refs):
    g = s_ref[0]
    sums, (keep_ref, got_ref, own_ref, oth_ref), outs = refs[:size], refs[size : size + 4], refs[size + 4 :]
    back_ref, go_ref, msgs, out_scratch = outs[0], outs[1], outs[2:-1], outs[-1]
    pre = sums[0][...]
    for p in sums[1:]:
        pre = pre + p[...]
    group = go_ref.shape[0]
    rows, per = size * group, group // boxes
    cot = jnp.concatenate([keep_ref[...], got_ref[...]], 1).astype(F32)
    small = jnp.concatenate([own_ref[...], oth_ref[...]], 1)
    step = HALVES * boxes
    phase, center_cot, offset_cot = (
        small[i * step + part * boxes : i * step + (part + 1) * boxes] for i in range(3)
    )
    bias = small[3 * step : 3 * step + 1]
    where = [[q * group + b * per for q in range(size)] for b in range(boxes)]
    radius, cross = [], []
    for b in range(boxes):
        radius.append(sum(jnp.sum(jnp.abs(pre[r : r + per]), 0, keepdims=True) for r in where[b]))
        cross.append(sum(jnp.sum(cot[r : r + per] * pre[r : r + per], 0, keepdims=True) for r in where[b]))
    radius, cross = jnp.concatenate(radius, 0), jnp.concatenate(cross, 0)
    center_pre = pre[rows : rows + boxes] + bias
    (slope, center_out, offset), pull = jax.vjp(lambda a, b: neuron(a, b, phase), center_pre, radius)
    g_center, g_radius = pull((cross, center_cot, offset_cot))
    for b in range(boxes):
        sl, gr = slope[b : b + 1], g_radius[b : b + 1]
        for r in where[b]:
            x = pre[r : r + per]
            sign = jnp.where(x > 0, gr, jnp.where(x < 0, -gr, 0.0))
            back_ref[r : r + per, :] = (sl * cot[r : r + per] + sign).astype(BF)
            out_scratch[r : r + per, :] = (sl * x).astype(BF)
    tail = []
    for value in (g_center, center_out, offset):
        high = value.astype(BF).astype(F32)
        tail += [high, value - high]
    tail.append(jnp.zeros((CENTER_ROWS - 6 * boxes, value.shape[1]), F32))
    back_ref[rows:, :] = jnp.concatenate(tail, 0).astype(BF)
    go_ref[...] = out_scratch[rows_at(g, group), :]
    for k, msg in zip(ORDER[1:], msgs):
        msg[: rows + CENTER_ROWS, :] = back_ref[...]
        msg[rows + CENTER_ROWS :, :] = out_scratch[rows_at(g ^ k, group), :]


def spread_kernel(s_ref, back_ref, go_ref, *refs):
    g = s_ref[0]
    msgs, (own_ref, oth_ref, far_ref, out_ref) = refs[:3], refs[3:]
    rows, lanes = back_ref.shape[0], back_ref.shape[1] // 2
    for i, k in enumerate(ORDER):
        at = rows_at(g ^ k, lanes)
        back, out = (back_ref, go_ref[...]) if i == 0 else (msgs[i - 1], msgs[i - 1][rows:, :])
        own_ref[:, at] = back[:rows, :lanes]
        oth_ref[:rows, at] = back[:rows, lanes:]
        far_ref[:, at] = back[:rows, lanes:]
        oth_ref[rows:, at] = out[:, lanes:]
        out_ref[:, at] = out[:, :lanes]


def input_grad_kernel(s_ref, back_ref, *refs):
    g, c, x = s_ref[0], s_ref[1], s_ref[2] >> 1
    msgs, w_ref, outs, res = refs[:3], refs[3], refs[4:-1], refs[-1]
    rows = back_ref.shape[0]
    over = (((1,), (1,)), ((), ()))
    total = None
    for i, k in enumerate(ORDER):
        back = back_ref[...] if i == 0 else msgs[i - 1][:rows, :]
        part = lax.dot_general(back, w_ref[g ^ k], over, preferred_element_type=F32)
        total = part if total is None else total + part
    res[...] = total
    group = (rows - CENTER_ROWS) // 4
    tail = res[4 * group : 4 * group + 8, :]
    for side, out in ((1 - x, outs[0]), (x, outs[1])):
        first = res[rows_at(side + 2 * c, group), :]
        second = res[rows_at(side + 2 * (1 - c), group), :]
        out[...] = jnp.concatenate([first, second, tail], 0).astype(out.dtype)


def input_both_kernel(s_ref, keep_ref, far_ref, first_ref, last_ref):
    group = (keep_ref.shape[0] - 8) // 2
    total = keep_ref[...] + far_ref[...].astype(F32)
    tail = total[2 * group :]
    first_ref[...] = jnp.concatenate([total[:group], tail], 0).astype(BF)
    last_ref[...] = jnp.concatenate([total[group : 2 * group], tail], 0).astype(BF)


def input_final_kernel(boxes, s_ref, *refs):
    msgs, (grad_ref, center_ref) = refs[:-2], refs[-2:]
    first = s_ref[0] >> 1
    per = grad_ref.shape[1]
    group = boxes * per
    rows = [[], []]
    for h in range(HALVES):
        for k in range(2):
            value = msgs[k][h * (group + 8) : (h + 1) * (group + 8), :].astype(F32)
            at = (first ^ k) * (HALVES * boxes) + h * boxes
            grad_ref[pl.ds(at, boxes)] = value[:group].reshape(boxes, per, -1)
            rows[k].append(value[group : group + boxes])
    near, far = (jnp.concatenate(r, 0) for r in rows)
    center_ref[...] = jnp.where(
        first == 0, jnp.concatenate([near, far], 0), jnp.concatenate([far, near], 0)
    )


def stack_kernel(s_ref, *refs):
    lefts, out = refs[:-1], refs[-1]
    rows = lefts[0].shape[0] // HALVES
    gens = rows - CENTER_ROWS
    tails = []
    for i in range(len(lefts) * HALVES):
        ref, h = lefts[i // HALVES], i % HALVES
        out[:, i * gens : (i + 1) * gens] = ref[h * rows : h * rows + gens, :].T
        tails.append(ref[h * rows + gens : (h + 1) * rows, :])
    width = out.shape[1] - len(lefts) * HALVES * gens
    pad = jnp.zeros((width - len(tails) * CENTER_ROWS, out.shape[0]), BF)
    out[:, len(tails) * gens :] = jnp.concatenate(tails + [pad], 0).T


def weight_grad_kernel(boxes, s_ref, after_ref, left_ref, *refs):
    rights, keeps, refs = refs[: 4 * HALVES], refs[4 * HALVES : 5 * HALVES], refs[5 * HALVES :]
    weight_ref, bias_ref, center_ref, offset_ref, gens_ref, done_ref, stack = refs
    per = gens_ref.shape[1]
    cols = weight_ref.shape[1]
    gens = rights[-1].shape[0] - CENTER_ROWS

    @pl.when(pl.program_id(0) == 0)
    def _():
        c = s_ref[1]
        done_ref[...] = jnp.zeros(done_ref.shape, F32)
        tails = []
        for i, right in enumerate(rights):
            stack[i * gens : (i + 1) * gens, :] = right[:gens, :cols]
            tail = right[gens : gens + CENTER_ROWS, :cols]
            at = len(rights) * gens + i * CENTER_ROWS
            stack[at : at + CENTER_ROWS, :] = tail
            tails.append(tail.astype(F32))
        used = len(rights) * (gens + CENTER_ROWS)
        if used < stack.shape[0]:
            stack[used:, :] = jnp.zeros((stack.shape[0] - used, cols), BF)
        bias_ref[...] = sum(jnp.sum(t[: 2 * boxes], 0, keepdims=True) for t in tails)
        for at, ref in ((2, center_ref), (4, offset_ref)):
            both = [
                t[at * boxes : (at + 1) * boxes] + t[(at + 1) * boxes : (at + 2) * boxes]
                for t in tails[: 2 * HALVES]
            ]
            mine, other = (jnp.concatenate(both[i * HALVES : (i + 1) * HALVES], 0) for i in range(2))
            ref[...] = jnp.where(
                c == 0, jnp.concatenate([mine, other], 0), jnp.concatenate([other, mine], 0)
            )
        for h in range(HALVES):
            for at, out in ((c, keeps[h][...]), (1 - c, rights[HALVES + h][gens + CENTER_ROWS :, :])):
                at = at * (HALVES * boxes) + h * boxes
                gens_ref[pl.ds(at, boxes)] = out.reshape(boxes, per, -1)

    weight_ref[...] = jnp.dot(left_ref[...], stack[...], preferred_element_type=F32)


def square_body(size, gens, center, weight, bias, phase, gens_cot, center_cot, offset_cot):
    box_dev, per_gen, width = gens.shape
    depth, cols = weight.shape
    core_boxes = box_dev // 2
    boxes = core_boxes // HALVES
    group = boxes * per_gen
    rows = size * group
    work = rows + CENTER_ROWS
    lanes = cols // size
    g, n = lax.axis_index("gen"), lax.axis_index("neur")
    c = n % 2
    scalars = jnp.stack([g, c, n, lax.axis_index("box")]).astype(jnp.int32)
    halves = range(HALVES)

    def over_gen(pieces):
        return [pieces[0]] + [
            lax.ppermute(piece, "gen", [(i, i ^ k) for i in range(size)])
            for piece, k in zip(pieces[1:], ORDER[1:])
        ]

    def over_core(x):
        return lax.ppermute(x, "neur", [(i, i ^ 1) for i in range(size)])

    def over_x(x):
        return lax.ppermute(x, "neur", [(i, i ^ 2) for i in range(size)])

    def over_box(x):
        return lax.ppermute(x, "box", [(0, 1), (1, 0)])

    def over_both(x):
        pairs = [(i * 2 + j, (i ^ 1) * 2 + (j ^ 1)) for i in range(size) for j in range(2)]
        return lax.ppermute(x, ("neur", "box"), pairs)

    def turned(x, k):
        pairs = [
            (i * size + j, ((j >> 1) + 2 * ((j & 1) ^ k)) * size + i)
            for i in range(size)
            for j in range(size)
        ]
        return lax.ppermute(x, ("gen", "neur"), pairs)

    anywhere = pl.BlockSpec(memory_space=pl.ANY)
    def held(x, *after):
        if not after:
            return x
        return call(copy_kernel, scalars, [x], [whole(x)], [shape(x.shape, x.dtype)], after=after)[0]

    with jax.named_scope("exchange_generators"):
        cot_rows = box_dev * per_gen * lanes // depth
        msgs = call(
            functools.partial(fold_kernel, size),
            scalars,
            [gens, gens_cot],
            [anywhere] * 2,
            [shape((core_boxes * per_gen + cot_rows, depth), BF)] * size,
            [pltpu.VMEM(gens_cot.shape, BF), pltpu.SemaphoreType.DMA((size * core_boxes + 1,))],
        )
        recv = over_gen(msgs)
    with jax.named_scope("swap_cores"):
        w_other = over_core(weight)
        (w_chunks,) = call(
            chunk_kernel,
            scalars,
            [weight, w_other],
            [whole(weight), whole(w_other)],
            [shape((size, depth, 2 * lanes), BF)],
            after=[recv[1]],
        )
        stacked = jnp.stack([phase.astype(F32), center_cot, offset_cot])

        def small(core):
            part = lax.dynamic_slice_in_dim(stacked, core * core_boxes, core_boxes, 1)
            pad = jnp.zeros((8 - 3 * core_boxes - 1, cols), F32)
            return jnp.concatenate([part.reshape(3 * core_boxes, cols), bias[None], pad], 0)

        small_own = small(c)
        small_oth = over_core(small(1 - c))
    with jax.named_scope("forward"):
        a_own, cot_keep, cot_send, *products = call(
            functools.partial(forward_kernel, size),
            scalars,
            [center, w_chunks, *recv],
            [
                pl.BlockSpec((box_dev, depth), lambda i, s: (0, s[0])),
                whole(w_chunks),
                *[whole(r) for r in recv],
            ],
            [shape((HALVES * work, depth), BF)]
            + [shape((HALVES * rows, lanes), BF)] * 2
            + [shape((rows + 8, 2 * lanes), F32)] * (HALVES * size),
        )
    with jax.named_scope("sum_products"):
        sums = []
        for h in halves:
            sums.append(over_gen(products[h * size : (h + 1) * size]))
        cot_got = over_core(cot_send)
    with jax.named_scope("share_generators"):
        a_box = over_box(a_own)
        pieces = [a_own, over_core(a_own), a_box, over_core(a_box)]
        (left,) = call(
            stack_kernel,
            scalars,
            pieces,
            [whole(v) for v in pieces],
            [shape((depth, 4 * HALVES * rows + 128), BF)],
        )
    keeps, sends = [], []
    small_spec = pl.BlockSpec((8, lanes), lambda i, s: (0, s[0]))
    for h in halves:
        cot_part = pl.BlockSpec((rows, lanes), lambda i, s, h=h: (h, 0))
        with jax.named_scope("relax"):
            back, go, *msgs = call(
                functools.partial(relax_kernel, size, boxes, h),
                scalars,
                [*sums[h], cot_keep, cot_got, small_own, small_oth],
                [*[whole(p) for p in sums[h]], cot_part, cot_part, small_spec, small_spec],
                [
                    shape((work, 2 * lanes), BF),
                    shape((group, 2 * lanes), BF),
                    *[shape((work + group, 2 * lanes), BF)] * (size - 1),
                ],
                [pltpu.VMEM((rows, 2 * lanes), BF)],
            )
        with jax.named_scope("exchange_back"):
            got = over_gen([None, *msgs])[1:]
            both = group + 8
            part = group + both
            send, keep = call(
                input_grad_kernel,
                scalars,
                [back, *got, w_chunks],
                [whole(v) for v in (back, *got, w_chunks)],
                [shape((part, depth), BF), shape((part, depth), F32)],
                [pltpu.VMEM((work, depth), F32)],
            )
            own, oth, oth_back, out_own = call(
                spread_kernel,
                scalars,
                [back, go, *got],
                [whole(v) for v in (back, go, *got)],
                [
                    shape((work, cols), BF),
                    shape((work + group, cols), BF),
                    shape((work, cols), BF),
                    shape((group, cols), BF),
                ],
                after=[send],
            )
            core_part = over_core(oth)
            keeps.append(out_own)
    with jax.named_scope("input_gradient"):

        far = over_x(send)
        first, last = call(
            input_both_kernel,
            scalars,
            [keep, far],
            [whole(keep), whole(far)],
            [shape((both, depth), BF)] * 2,
        )
        finals = [turned(first, 0), turned(last, 1)]
        rights = [own, core_part, over_box(own), held(over_both(oth_back), last)]
    with jax.named_scope("weight_gradient"):
        blocks = 4
        out_shape = [
            shape((depth, cols), F32),
            shape((1, cols), F32),
            shape((box_dev, cols), F32),
            shape((box_dev, cols), F32),
            shape((box_dev, per_gen, cols), BF),
            shape((8, 128), F32),
        ]
        weight_grad, bias_grad, center_out, offset, gens_out, done = pl.pallas_call(
            functools.partial(weight_grad_kernel, boxes),
            grid_spec=pltpu.PrefetchScalarGridSpec(
                num_scalar_prefetch=1,
                grid=(blocks,),
                in_specs=[anywhere, pl.BlockSpec((depth // blocks, left.shape[1]), lambda i, s: (i, 0))]
                + [whole(r) for r in rights + keeps],
                out_specs=[pl.BlockSpec((depth // blocks, cols), lambda i, s: (i, 0))]
                + [whole(o) for o in out_shape[1:]],
                scratch_shapes=[pltpu.VMEM((left.shape[1], cols), BF)],
            ),
            out_shape=out_shape,
            compiler_params=params(),
        )(scalars, last, left, *rights, *keeps)
    with jax.named_scope("input_gradient"):
        gens_grad, center_grad = call(
            functools.partial(input_final_kernel, boxes),
            scalars,
            finals,
            [whole(r) for r in finals],
            [shape((box_dev, per_gen, depth), F32), shape((box_dev, depth), F32)],
            after=[done],
        )
    return (
        center_out,
        gens_out,
        offset,
        weight_grad,
        bias_grad.reshape(cols),
        gens_grad,
        center_grad,
    )


def solution(mesh):
    sizes = dict(mesh.shape)

    def run(gens, center, weight, bias, phase, gens_cot, center_cot, offset_cot):
        size = sizes["gen"]
        box_dev = gens.shape[0] // sizes["box"]
        per_gen = gens.shape[1] // size
        cols = weight.shape[1] // sizes["neur"]
        square = (
            size == sizes["neur"] == 4
            and sizes["box"] == 2
            and box_dev == 4
            and per_gen % 16 == 0
            and cols % (128 * size) == 0
            and weight.shape[0] % (1024 * size) == 0
        )
        body = functools.partial(square_body, size) if square else general_body
        return jax.shard_map(
            body,
            mesh=mesh,
            in_specs=(
                P("box", "gen", None),
                P("box", None),
                P("gen", "neur"),
                P("neur"),
                P("box", "neur"),
                P("box", "gen", "neur"),
                P("box", "neur"),
                P("box", "neur"),
            ),
            out_specs=(
                P("box", "neur"),
                P("box", "gen", "neur"),
                P("box", "neur"),
                P("gen", "neur"),
                P("neur"),
                P("box", "gen", "neur"),
                P("box", "neur"),
            ),
            check_vma=False,
        )(gens, center, weight, bias, phase, gens_cot, center_cot, offset_cot)

    return run
```

```python
import functools

import jax
import jax.numpy as jnp
from jax import lax
from jax.experimental import pallas as pl
from jax.experimental.pallas import tpu as pltpu
from jax.sharding import PartitionSpec as P

BF = jnp.bfloat16
F32 = jnp.float32
VMEM_LIMIT = 32 * 1024 * 1024


def neuron(center_pre, radius, phase):
    upper = center_pre + radius
    lower = center_pre - radius
    ratio = jnp.clip(upper / (upper - lower + 1e-05), 0.0, 1.0)
    active = (phase == 1).astype(center_pre.dtype)
    crossing = (phase == 2).astype(center_pre.dtype)
    slope = active + crossing * ratio
    offset = crossing * (-ratio * lower * 0.5)
    return (slope, slope * center_pre + offset, offset)


def general_body(gens, center, weight, bias, phase, gens_cot, center_cot, offset_cot):
    box_dev, gen_dev, width = gens.shape
    local_cols = weight.shape[1]
    local_rows = box_dev * gen_dev
    wide = jnp.concatenate([gens.reshape(local_rows, width), center], 0)
    full_weight = lax.all_gather(weight, "gen", axis=0, tiled=True)
    product = jnp.dot(wide, full_weight, preferred_element_type=F32)
    gen_pre = product[:local_rows].reshape(box_dev, gen_dev, local_cols)
    center_pre = product[local_rows:] + bias
    part_radius = jnp.sum(jnp.abs(gen_pre), axis=1)
    cot_wide = gens_cot.astype(F32)
    radius = lax.psum(part_radius, "gen")
    slope, center_out, offset = neuron(center_pre, radius, phase)
    gens_out = (slope[:, None, :] * gen_pre).astype(BF)
    intersection = lax.psum(jnp.sum(cot_wide * gen_pre, axis=1), "gen")
    unused, pull = jax.vjp(lambda a, b: neuron(a, b, phase), center_pre, radius)
    g_center, g_radius = pull((intersection, center_cot, offset_cot))
    gen_back = (slope[:, None, :] * cot_wide + jnp.sign(gen_pre) * g_radius[:, None, :]).astype(BF)
    center_back = g_center.astype(BF)
    back = jnp.concatenate([gen_back.reshape(local_rows, local_cols), center_back], 0)
    first_gen = (lax.axis_index("gen") == 0).astype(BF)
    back_owned = jnp.concatenate(
        [gen_back.reshape(local_rows, local_cols), center_back * first_gen], 0
    )
    shares = lax.psum_scatter(
        lax.dot_general(wide, back_owned, (((0,), (0,)), ((), ())), preferred_element_type=F32),
        ("gen", "box"),
        scatter_dimension=0,
        tiled=True,
    )
    weight_grad = lax.all_gather(shares, "box", axis=0, tiled=True)
    bias_grad = lax.psum(jnp.sum(g_center, axis=0), "box")
    partial_back = lax.dot_general(
        back, full_weight, (((1,), (1,)), ((), ())), preferred_element_type=F32
    )
    summed = lax.psum_scatter(partial_back, "neur", scatter_dimension=1, tiled=True)
    gens_grad = summed[:local_rows].reshape(box_dev, gen_dev, summed.shape[1])
    center_grad = summed[local_rows:]
    return (center_out, gens_out, offset, weight_grad, bias_grad, gens_grad, center_grad)


CENTER_ROWS = 16
HALVES = 1
ORDER = (0, 3, 2, 1)
BACK_ORDER = (0, 2, 3, 1)
COSTS = {"fold": 1000000, "copy": 1000000000, "forward": 1000000000, "relax": 1000000000, "input_both": 300000000}


def params():
    return pltpu.CompilerParams(vmem_limit_bytes=VMEM_LIMIT)


def shape(dims, dtype):
    return jax.ShapeDtypeStruct(dims, dtype)


def whole(x):
    return pl.BlockSpec(x.shape, lambda i, s, r=len(x.shape): (0,) * r)


def call(kernel, scalars, args, specs, outs, scratch=(), after=()):
    skip = len(after)
    cost = COSTS.get(getattr(kernel, "func", kernel).__name__.replace("_kernel", ""))

    def body(s_ref, *refs):
        kernel(s_ref, *refs[skip:])

    return pl.pallas_call(
        body,
        grid_spec=pltpu.PrefetchScalarGridSpec(
            num_scalar_prefetch=1,
            grid=(1,),
            in_specs=[pl.BlockSpec(memory_space=pl.ANY)] * skip + specs,
            out_specs=[whole(o) for o in outs],
            scratch_shapes=list(scratch),
        ),
        out_shape=outs,
        compiler_params=params(),
        cost_estimate=pl.CostEstimate(flops=cost, bytes_accessed=1 << 20, transcendentals=0) if cost else None,
    )(scalars, *after, *args)


def rows_at(index, size):
    return pl.ds(pl.multiple_of(index * size, size), size)


def fold_kernel(size, s_ref, gens_ref, cot_ref, *refs):
    g, c = s_ref[0], s_ref[1]
    outs, cot, sems = refs[:size], refs[-2], refs[-1]
    core_boxes, per_gen = gens_ref.shape[0] // 2, gens_ref.shape[1]
    depth = outs[0].shape[1]
    copies = [pltpu.make_async_copy(cot_ref, cot, sems.at[0])]
    for k, out in zip(ORDER, outs):
        for b in range(core_boxes):
            source = gens_ref.at[c * core_boxes + b, :, rows_at(g ^ k, depth)]
            target = out.at[pl.ds(b * per_gen, per_gen), :]
            copies.append(pltpu.make_async_copy(source, target, sems.at[len(copies)]))
    for copy in copies:
        copy.start()
    for copy in copies:
        copy.wait()
    rows, lanes = core_boxes * per_gen, cot.shape[2] // size
    for k, out in zip(ORDER, outs):
        value = cot[:, :, rows_at(g ^ k, lanes)].reshape(-1, lanes)
        per = out.shape[0] - rows
        for i in range(value.shape[0] // per):
            out[rows:, i * lanes : (i + 1) * lanes] = value[i * per : (i + 1) * per]


def chunk_kernel(s_ref, own_ref, oth_ref, out_ref):
    lanes = out_ref.shape[2] // 2
    for j in range(out_ref.shape[0]):
        out_ref[j, :, :lanes] = own_ref[:, j * lanes : (j + 1) * lanes]
        out_ref[j, :, lanes:] = oth_ref[:, j * lanes : (j + 1) * lanes]


def copy_kernel(s_ref, in_ref, out_ref):
    out_ref[...] = in_ref[...]


def forward_kernel(size, s_ref, center_ref, w_ref, *refs):
    g, c = s_ref[0], s_ref[1]
    recv, (a_ref, keep_ref, send_ref), products = refs[:size], refs[size : size + 3], refs[size + 3 :]
    work, depth = a_ref.shape[0] // HALVES, a_ref.shape[1]
    group = (work - CENTER_ROWS) // size
    mid = center_ref[...].astype(F32)
    core_boxes = mid.shape[0] // 2
    boxes = core_boxes // HALVES
    mid = jnp.where(c == 0, mid[:core_boxes], mid[core_boxes:])
    pad = jnp.zeros((CENTER_ROWS - boxes, depth), F32)
    lanes = products[0].shape[1] // 2
    for h in range(HALVES):
        for k, msg in zip(ORDER, recv):
            at = pl.ds(pl.multiple_of(h * work + (g ^ k) * group, CENTER_ROWS), group)
            a_ref[at, :] = msg[h * group : (h + 1) * group, :]
        tail = jnp.concatenate([mid[h * boxes : (h + 1) * boxes], pad], 0).astype(BF)
        a_ref[(h + 1) * work - CENTER_ROWS : (h + 1) * work, :] = tail
    a = a_ref[...]
    for i, k in enumerate(ORDER):
        product = jnp.dot(a, w_ref[g ^ k], preferred_element_type=F32)
        for h in range(HALVES):
            out = products[h * size + i]
            out[...] = product[h * work : h * work + out.shape[0]]
    rows = HALVES * group
    for k, msg in zip(ORDER, recv):
        cot = [msg[rows:, i * lanes : (i + 1) * lanes] for i in range(depth // lanes)]
        cot = jnp.concatenate(cot, 0)
        low, high = cot[:rows], cot[rows:]
        for ref, value in (
            (keep_ref, jnp.where(c == 0, low, high)),
            (send_ref, jnp.where(c == 0, high, low)),
        ):
            for h in range(HALVES):
                at = pl.ds(pl.multiple_of(h * size * group + (g ^ k) * group, group), group)
                ref[at, :] = value[h * group : (h + 1) * group]


def relax_kernel(size, boxes, part, s_ref, *refs):
    g = s_ref[0]
    sums, (keep_ref, got_ref, own_ref, oth_ref), outs = refs[:size], refs[size : size + 4], refs[size + 4 :]
    back_ref, go_ref, msgs, out_scratch = outs[0], outs[1], outs[2:-1], outs[-1]
    pre = sums[0][...]
    for p in sums[1:]:
        pre = pre + p[...]
    group = go_ref.shape[0]
    rows, per = size * group, group // boxes
    cot = jnp.concatenate([keep_ref[...], got_ref[...]], 1).astype(F32)
    small = jnp.concatenate([own_ref[...], oth_ref[...]], 1)
    step = HALVES * boxes
    phase, center_cot, offset_cot = (
        small[i * step + part * boxes : i * step + (part + 1) * boxes] for i in range(3)
    )
    bias = small[3 * step : 3 * step + 1]
    where = [[q * group + b * per for q in range(size)] for b in range(boxes)]
    radius, cross = [], []
    for b in range(boxes):
        radius.append(sum(jnp.sum(jnp.abs(pre[r : r + per]), 0, keepdims=True) for r in where[b]))
        cross.append(sum(jnp.sum(cot[r : r + per] * pre[r : r + per], 0, keepdims=True) for r in where[b]))
    radius, cross = jnp.concatenate(radius, 0), jnp.concatenate(cross, 0)
    center_pre = pre[rows : rows + boxes] + bias
    (slope, center_out, offset), pull = jax.vjp(lambda a, b: neuron(a, b, phase), center_pre, radius)
    g_center, g_radius = pull((cross, center_cot, offset_cot))
    for b in range(boxes):
        sl, gr = slope[b : b + 1], g_radius[b : b + 1]
        for r in where[b]:
            x = pre[r : r + per]
            sign = jnp.where(x > 0, gr, jnp.where(x < 0, -gr, 0.0))
            back_ref[r : r + per, :] = (sl * cot[r : r + per] + sign).astype(BF)
            out_scratch[r : r + per, :] = (sl * x).astype(BF)
    tail = []
    for value in (g_center, center_out, offset):
        high = value.astype(BF).astype(F32)
        tail += [high, value - high]
    tail.append(jnp.zeros((CENTER_ROWS - 6 * boxes, value.shape[1]), F32))
    back_ref[rows:, :] = jnp.concatenate(tail, 0).astype(BF)
    go_ref[...] = out_scratch[rows_at(g, group), :]
    for k, msg in zip(BACK_ORDER[1:], msgs):
        msg[: rows + CENTER_ROWS, :] = back_ref[...]
        msg[rows + CENTER_ROWS :, :] = out_scratch[rows_at(g ^ k, group), :]


def spread_kernel(s_ref, back_ref, go_ref, *refs):
    g = s_ref[0]
    msgs, (own_ref, oth_ref, far_ref, out_ref) = refs[:3], refs[3:]
    rows, lanes = back_ref.shape[0], back_ref.shape[1] // 2
    for i, k in enumerate(BACK_ORDER):
        at = rows_at(g ^ k, lanes)
        back, out = (back_ref, go_ref[...]) if i == 0 else (msgs[i - 1], msgs[i - 1][rows:, :])
        own_ref[:, at] = back[:rows, :lanes]
        oth_ref[:rows, at] = back[:rows, lanes:]
        far_ref[:, at] = back[:rows, lanes:]
        oth_ref[rows:, at] = out[:, lanes:]
        out_ref[:, at] = out[:, :lanes]


def input_grad_kernel(s_ref, back_ref, *refs):
    g, c, x = s_ref[0], s_ref[1], s_ref[2] >> 1
    msgs, w_ref, outs, res = refs[:3], refs[3], refs[4:-1], refs[-1]
    rows = back_ref.shape[0]
    over = (((1,), (1,)), ((), ()))
    total = None
    for i, k in enumerate(BACK_ORDER):
        back = back_ref[...] if i == 0 else msgs[i - 1][:rows, :]
        part = lax.dot_general(back, w_ref[g ^ k], over, preferred_element_type=F32)
        total = part if total is None else total + part
    res[...] = total
    group = (rows - CENTER_ROWS) // 4
    tail = res[4 * group : 4 * group + 8, :]
    for side, out in ((1 - x, outs[0]), (x, outs[1])):
        first = res[rows_at(side + 2 * c, group), :]
        second = res[rows_at(side + 2 * (1 - c), group), :]
        out[...] = jnp.concatenate([first, second, tail], 0).astype(out.dtype)


def input_both_kernel(s_ref, keep_ref, far_ref, first_ref, last_ref):
    group = (keep_ref.shape[0] - 8) // 2
    total = keep_ref[...] + far_ref[...].astype(F32)
    tail = total[2 * group :]
    first_ref[...] = jnp.concatenate([total[:group], tail], 0).astype(BF)
    last_ref[...] = jnp.concatenate([total[group : 2 * group], tail], 0).astype(BF)


def input_final_kernel(boxes, s_ref, *refs):
    msgs, (grad_ref, center_ref) = refs[:-2], refs[-2:]
    first = s_ref[0] >> 1
    per = grad_ref.shape[1]
    group = boxes * per
    rows = [[], []]
    for h in range(HALVES):
        for k in range(2):
            value = msgs[k][h * (group + 8) : (h + 1) * (group + 8), :].astype(F32)
            at = (first ^ k) * (HALVES * boxes) + h * boxes
            grad_ref[pl.ds(at, boxes)] = value[:group].reshape(boxes, per, -1)
            rows[k].append(value[group : group + boxes])
    near, far = (jnp.concatenate(r, 0) for r in rows)
    center_ref[...] = jnp.where(
        first == 0, jnp.concatenate([near, far], 0), jnp.concatenate([far, near], 0)
    )


def stack_kernel(s_ref, *refs):
    lefts, out = refs[:-1], refs[-1]
    rows = lefts[0].shape[0] // HALVES
    gens = rows - CENTER_ROWS
    tails = []
    for i in range(len(lefts) * HALVES):
        ref, h = lefts[i // HALVES], i % HALVES
        out[:, i * gens : (i + 1) * gens] = ref[h * rows : h * rows + gens, :].T
        tails.append(ref[h * rows + gens : (h + 1) * rows, :])
    width = out.shape[1] - len(lefts) * HALVES * gens
    pad = jnp.zeros((width - len(tails) * CENTER_ROWS, out.shape[0]), BF)
    out[:, len(tails) * gens :] = jnp.concatenate(tails + [pad], 0).T


def weight_grad_kernel(boxes, s_ref, after_ref, left_ref, *refs):
    rights, keeps, refs = refs[: 4 * HALVES], refs[4 * HALVES : 5 * HALVES], refs[5 * HALVES :]
    weight_ref, bias_ref, center_ref, offset_ref, gens_ref, done_ref, stack = refs
    per = gens_ref.shape[1]
    cols = weight_ref.shape[1]
    gens = rights[-1].shape[0] - CENTER_ROWS

    @pl.when(pl.program_id(0) == 0)
    def _():
        c = s_ref[1]
        done_ref[...] = jnp.zeros(done_ref.shape, F32)
        tails = []
        for i, right in enumerate(rights):
            stack[i * gens : (i + 1) * gens, :] = right[:gens, :cols]
            tail = right[gens : gens + CENTER_ROWS, :cols]
            at = len(rights) * gens + i * CENTER_ROWS
            stack[at : at + CENTER_ROWS, :] = tail
            tails.append(tail.astype(F32))
        used = len(rights) * (gens + CENTER_ROWS)
        if used < stack.shape[0]:
            stack[used:, :] = jnp.zeros((stack.shape[0] - used, cols), BF)
        bias_ref[...] = sum(jnp.sum(t[: 2 * boxes], 0, keepdims=True) for t in tails)
        for at, ref in ((2, center_ref), (4, offset_ref)):
            both = [
                t[at * boxes : (at + 1) * boxes] + t[(at + 1) * boxes : (at + 2) * boxes]
                for t in tails[: 2 * HALVES]
            ]
            mine, other = (jnp.concatenate(both[i * HALVES : (i + 1) * HALVES], 0) for i in range(2))
            ref[...] = jnp.where(
                c == 0, jnp.concatenate([mine, other], 0), jnp.concatenate([other, mine], 0)
            )
        for h in range(HALVES):
            for at, out in ((c, keeps[h][...]), (1 - c, rights[HALVES + h][gens + CENTER_ROWS :, :])):
                at = at * (HALVES * boxes) + h * boxes
                gens_ref[pl.ds(at, boxes)] = out.reshape(boxes, per, -1)

    weight_ref[...] = jnp.dot(left_ref[...], stack[...], preferred_element_type=F32)


def square_body(size, gens, center, weight, bias, phase, gens_cot, center_cot, offset_cot):
    box_dev, per_gen, width = gens.shape
    depth, cols = weight.shape
    core_boxes = box_dev // 2
    boxes = core_boxes // HALVES
    group = boxes * per_gen
    rows = size * group
    work = rows + CENTER_ROWS
    lanes = cols // size
    g, n = lax.axis_index("gen"), lax.axis_index("neur")
    c = n % 2
    scalars = jnp.stack([g, c, n, lax.axis_index("box")]).astype(jnp.int32)
    halves = range(HALVES)

    def over_gen(pieces, order=ORDER):
        return [pieces[0]] + [
            lax.ppermute(piece, "gen", [(i, i ^ k) for i in range(size)])
            for piece, k in zip(pieces[1:], order[1:])
        ]

    def over_core(x):
        return lax.ppermute(x, "neur", [(i, i ^ 1) for i in range(size)])

    def over_x(x):
        return lax.ppermute(x, "neur", [(i, i ^ 2) for i in range(size)])

    def over_box(x):
        return lax.ppermute(x, "box", [(0, 1), (1, 0)])

    def over_both(x):
        pairs = [(i * 2 + j, (i ^ 1) * 2 + (j ^ 1)) for i in range(size) for j in range(2)]
        return lax.ppermute(x, ("neur", "box"), pairs)

    def turned(x, k):
        pairs = [
            (i * size + j, ((j >> 1) + 2 * ((j & 1) ^ k)) * size + i)
            for i in range(size)
            for j in range(size)
        ]
        return lax.ppermute(x, ("gen", "neur"), pairs)

    anywhere = pl.BlockSpec(memory_space=pl.ANY)
    def held(x, *after):
        if not after:
            return x
        return call(copy_kernel, scalars, [x], [whole(x)], [shape(x.shape, x.dtype)], after=after)[0]

    with jax.named_scope("exchange_generators"):
        cot_rows = box_dev * per_gen * lanes // depth
        msgs = call(
            functools.partial(fold_kernel, size),
            scalars,
            [gens, gens_cot],
            [anywhere] * 2,
            [shape((core_boxes * per_gen + cot_rows, depth), BF)] * size,
            [pltpu.VMEM(gens_cot.shape, BF), pltpu.SemaphoreType.DMA((size * core_boxes + 1,))],
        )
        recv = over_gen(msgs)
    with jax.named_scope("swap_cores"):
        w_other = over_core(weight)
        (w_chunks,) = call(
            chunk_kernel,
            scalars,
            [weight, w_other],
            [whole(weight), whole(w_other)],
            [shape((size, depth, 2 * lanes), BF)],
            after=[recv[1]],
        )
        stacked = jnp.stack([phase.astype(F32), center_cot, offset_cot])

        def small(core):
            part = lax.dynamic_slice_in_dim(stacked, core * core_boxes, core_boxes, 1)
            pad = jnp.zeros((8 - 3 * core_boxes - 1, cols), F32)
            return jnp.concatenate([part.reshape(3 * core_boxes, cols), bias[None], pad], 0)

        small_own = small(c)
        small_oth = over_core(small(1 - c))
    with jax.named_scope("forward"):
        a_own, cot_keep, cot_send, *products = call(
            functools.partial(forward_kernel, size),
            scalars,
            [center, w_chunks, *recv],
            [
                pl.BlockSpec((box_dev, depth), lambda i, s: (0, s[0])),
                whole(w_chunks),
                *[whole(r) for r in recv],
            ],
            [shape((HALVES * work, depth), BF)]
            + [shape((HALVES * rows, lanes), BF)] * 2
            + [shape((rows + 8, 2 * lanes), F32)] * (HALVES * size),
        )
    with jax.named_scope("sum_products"):
        sums = []
        for h in halves:
            sums.append(over_gen(products[h * size : (h + 1) * size]))
        cot_got = over_core(cot_send)
    with jax.named_scope("share_generators"):
        a_box = over_box(a_own)
        pieces = [a_own, over_core(a_own), a_box, over_core(a_box)]
        (left,) = call(
            stack_kernel,
            scalars,
            pieces,
            [whole(v) for v in pieces],
            [shape((depth, 4 * HALVES * rows + 128), BF)],
        )
    keeps, sends = [], []
    small_spec = pl.BlockSpec((8, lanes), lambda i, s: (0, s[0]))
    for h in halves:
        cot_part = pl.BlockSpec((rows, lanes), lambda i, s, h=h: (h, 0))
        with jax.named_scope("relax"):
            back, go, *msgs = call(
                functools.partial(relax_kernel, size, boxes, h),
                scalars,
                [*sums[h], cot_keep, cot_got, small_own, small_oth],
                [*[whole(p) for p in sums[h]], cot_part, cot_part, small_spec, small_spec],
                [
                    shape((work, 2 * lanes), BF),
                    shape((group, 2 * lanes), BF),
                    *[shape((work + group, 2 * lanes), BF)] * (size - 1),
                ],
                [pltpu.VMEM((rows, 2 * lanes), BF)],
            )
        with jax.named_scope("exchange_back"):
            got = over_gen([None, *msgs], BACK_ORDER)[1:]
            both = group + 8
            part = group + both
            send, keep = call(
                input_grad_kernel,
                scalars,
                [back, *got, w_chunks],
                [whole(v) for v in (back, *got, w_chunks)],
                [shape((part, depth), BF), shape((part, depth), F32)],
                [pltpu.VMEM((work, depth), F32)],
            )
            own, oth, oth_back, out_own = call(
                spread_kernel,
                scalars,
                [back, go, *got],
                [whole(v) for v in (back, go, *got)],
                [
                    shape((work, cols), BF),
                    shape((work + group, cols), BF),
                    shape((work, cols), BF),
                    shape((group, cols), BF),
                ],
                after=[send],
            )
            core_part = over_core(oth)
            keeps.append(out_own)
    with jax.named_scope("input_gradient"):

        far = over_x(send)
        first, last = call(
            input_both_kernel,
            scalars,
            [keep, far],
            [whole(keep), whole(far)],
            [shape((both, depth), BF)] * 2,
        )
        finals = [turned(first, 0), turned(last, 1)]
        rights = [own, core_part, over_box(own), held(over_both(oth_back), last)]
    with jax.named_scope("weight_gradient"):
        blocks = 4
        out_shape = [
            shape((depth, cols), F32),
            shape((1, cols), F32),
            shape((box_dev, cols), F32),
            shape((box_dev, cols), F32),
            shape((box_dev, per_gen, cols), BF),
            shape((8, 128), F32),
        ]
        weight_grad, bias_grad, center_out, offset, gens_out, done = pl.pallas_call(
            functools.partial(weight_grad_kernel, boxes),
            grid_spec=pltpu.PrefetchScalarGridSpec(
                num_scalar_prefetch=1,
                grid=(blocks,),
                in_specs=[anywhere, pl.BlockSpec((depth // blocks, left.shape[1]), lambda i, s: (i, 0))]
                + [whole(r) for r in rights + keeps],
                out_specs=[pl.BlockSpec((depth // blocks, cols), lambda i, s: (i, 0))]
                + [whole(o) for o in out_shape[1:]],
                scratch_shapes=[pltpu.VMEM((left.shape[1], cols), BF)],
            ),
            out_shape=out_shape,
            compiler_params=params(),
        )(scalars, last, left, *rights, *keeps)
    with jax.named_scope("input_gradient"):
        gens_grad, center_grad = call(
            functools.partial(input_final_kernel, boxes),
            scalars,
            finals,
            [whole(r) for r in finals],
            [shape((box_dev, per_gen, depth), F32), shape((box_dev, depth), F32)],
            after=[done],
        )
    return (
        center_out,
        gens_out,
        offset,
        weight_grad,
        bias_grad.reshape(cols),
        gens_grad,
        center_grad,
    )


def solution(mesh):
    sizes = dict(mesh.shape)

    def run(gens, center, weight, bias, phase, gens_cot, center_cot, offset_cot):
        size = sizes["gen"]
        box_dev = gens.shape[0] // sizes["box"]
        per_gen = gens.shape[1] // size
        cols = weight.shape[1] // sizes["neur"]
        square = (
            size == sizes["neur"] == 4
            and sizes["box"] == 2
            and box_dev == 4
            and per_gen % 16 == 0
            and cols % (128 * size) == 0
            and weight.shape[0] % (1024 * size) == 0
        )
        body = functools.partial(square_body, size) if square else general_body
        return jax.shard_map(
            body,
            mesh=mesh,
            in_specs=(
                P("box", "gen", None),
                P("box", None),
                P("gen", "neur"),
                P("neur"),
                P("box", "neur"),
                P("box", "gen", "neur"),
                P("box", "neur"),
                P("box", "neur"),
            ),
            out_specs=(
                P("box", "neur"),
                P("box", "gen", "neur"),
                P("box", "neur"),
                P("gen", "neur"),
                P("neur"),
                P("box", "gen", "neur"),
                P("box", "neur"),
            ),
            check_vma=False,
        )(gens, center, weight, bias, phase, gens_cot, center_cot, offset_cot)

    return run
```

```python
import functools

import jax
import jax.numpy as jnp
from jax import lax
from jax.experimental import pallas as pl
from jax.experimental.pallas import tpu as pltpu
from jax.sharding import PartitionSpec as P

BF = jnp.bfloat16
F32 = jnp.float32
VMEM_LIMIT = 32 * 1024 * 1024


def neuron(center_pre, radius, phase):
    upper = center_pre + radius
    lower = center_pre - radius
    ratio = jnp.clip(upper / (upper - lower + 1e-05), 0.0, 1.0)
    active = (phase == 1).astype(center_pre.dtype)
    crossing = (phase == 2).astype(center_pre.dtype)
    slope = active + crossing * ratio
    offset = crossing * (-ratio * lower * 0.5)
    return (slope, slope * center_pre + offset, offset)


def general_body(gens, center, weight, bias, phase, gens_cot, center_cot, offset_cot):
    box_dev, gen_dev, width = gens.shape
    local_cols = weight.shape[1]
    local_rows = box_dev * gen_dev
    wide = jnp.concatenate([gens.reshape(local_rows, width), center], 0)
    full_weight = lax.all_gather(weight, "gen", axis=0, tiled=True)
    product = jnp.dot(wide, full_weight, preferred_element_type=F32)
    gen_pre = product[:local_rows].reshape(box_dev, gen_dev, local_cols)
    center_pre = product[local_rows:] + bias
    part_radius = jnp.sum(jnp.abs(gen_pre), axis=1)
    cot_wide = gens_cot.astype(F32)
    radius = lax.psum(part_radius, "gen")
    slope, center_out, offset = neuron(center_pre, radius, phase)
    gens_out = (slope[:, None, :] * gen_pre).astype(BF)
    intersection = lax.psum(jnp.sum(cot_wide * gen_pre, axis=1), "gen")
    unused, pull = jax.vjp(lambda a, b: neuron(a, b, phase), center_pre, radius)
    g_center, g_radius = pull((intersection, center_cot, offset_cot))
    gen_back = (slope[:, None, :] * cot_wide + jnp.sign(gen_pre) * g_radius[:, None, :]).astype(BF)
    center_back = g_center.astype(BF)
    back = jnp.concatenate([gen_back.reshape(local_rows, local_cols), center_back], 0)
    first_gen = (lax.axis_index("gen") == 0).astype(BF)
    back_owned = jnp.concatenate(
        [gen_back.reshape(local_rows, local_cols), center_back * first_gen], 0
    )
    shares = lax.psum_scatter(
        lax.dot_general(wide, back_owned, (((0,), (0,)), ((), ())), preferred_element_type=F32),
        ("gen", "box"),
        scatter_dimension=0,
        tiled=True,
    )
    weight_grad = lax.all_gather(shares, "box", axis=0, tiled=True)
    bias_grad = lax.psum(jnp.sum(g_center, axis=0), "box")
    partial_back = lax.dot_general(
        back, full_weight, (((1,), (1,)), ((), ())), preferred_element_type=F32
    )
    summed = lax.psum_scatter(partial_back, "neur", scatter_dimension=1, tiled=True)
    gens_grad = summed[:local_rows].reshape(box_dev, gen_dev, summed.shape[1])
    center_grad = summed[local_rows:]
    return (center_out, gens_out, offset, weight_grad, bias_grad, gens_grad, center_grad)


CENTER_ROWS = 16
HALVES = 1
ORDER = (0, 3, 2, 1)
BACK_ORDER = (0, 2, 3, 1)
COSTS = {"fold": 1000000, "copy": 1000000000, "forward": 1000000000, "relax": 1000000000, "input_both": 300000000, "input_final": 1000000000}


def params():
    return pltpu.CompilerParams(vmem_limit_bytes=VMEM_LIMIT)


def shape(dims, dtype):
    return jax.ShapeDtypeStruct(dims, dtype)


def whole(x):
    return pl.BlockSpec(x.shape, lambda i, s, r=len(x.shape): (0,) * r)


def call(kernel, scalars, args, specs, outs, scratch=(), after=()):
    skip = len(after)
    cost = COSTS.get(getattr(kernel, "func", kernel).__name__.replace("_kernel", ""))

    def body(s_ref, *refs):
        kernel(s_ref, *refs[skip:])

    return pl.pallas_call(
        body,
        grid_spec=pltpu.PrefetchScalarGridSpec(
            num_scalar_prefetch=1,
            grid=(1,),
            in_specs=[pl.BlockSpec(memory_space=pl.ANY)] * skip + specs,
            out_specs=[whole(o) for o in outs],
            scratch_shapes=list(scratch),
        ),
        out_shape=outs,
        compiler_params=params(),
        cost_estimate=pl.CostEstimate(flops=cost, bytes_accessed=1 << 20, transcendentals=0) if cost else None,
    )(scalars, *after, *args)


def rows_at(index, size):
    return pl.ds(pl.multiple_of(index * size, size), size)


def fold_kernel(size, s_ref, gens_ref, cot_ref, *refs):
    g, c = s_ref[0], s_ref[1]
    outs, cot, sems = refs[:size], refs[-2], refs[-1]
    core_boxes, per_gen = gens_ref.shape[0] // 2, gens_ref.shape[1]
    depth = outs[0].shape[1]
    copies = [pltpu.make_async_copy(cot_ref, cot, sems.at[0])]
    for k, out in zip(ORDER, outs):
        for b in range(core_boxes):
            source = gens_ref.at[c * core_boxes + b, :, rows_at(g ^ k, depth)]
            target = out.at[pl.ds(b * per_gen, per_gen), :]
            copies.append(pltpu.make_async_copy(source, target, sems.at[len(copies)]))
    for copy in copies:
        copy.start()
    for copy in copies:
        copy.wait()
    rows, lanes = core_boxes * per_gen, cot.shape[2] // size
    for k, out in zip(ORDER, outs):
        value = cot[:, :, rows_at(g ^ k, lanes)].reshape(-1, lanes)
        per = out.shape[0] - rows
        for i in range(value.shape[0] // per):
            out[rows:, i * lanes : (i + 1) * lanes] = value[i * per : (i + 1) * per]


def chunk_kernel(s_ref, own_ref, oth_ref, out_ref):
    lanes = out_ref.shape[2] // 2
    for j in range(out_ref.shape[0]):
        out_ref[j, :, :lanes] = own_ref[:, j * lanes : (j + 1) * lanes]
        out_ref[j, :, lanes:] = oth_ref[:, j * lanes : (j + 1) * lanes]


def copy_kernel(s_ref, in_ref, out_ref):
    out_ref[...] = in_ref[...]


def forward_kernel(size, s_ref, center_ref, w_ref, *refs):
    g, c = s_ref[0], s_ref[1]
    recv, (a_ref, keep_ref, send_ref), products = refs[:size], refs[size : size + 3], refs[size + 3 :]
    work, depth = a_ref.shape[0] // HALVES, a_ref.shape[1]
    group = (work - CENTER_ROWS) // size
    mid = center_ref[...].astype(F32)
    core_boxes = mid.shape[0] // 2
    boxes = core_boxes // HALVES
    mid = jnp.where(c == 0, mid[:core_boxes], mid[core_boxes:])
    pad = jnp.zeros((CENTER_ROWS - boxes, depth), F32)
    lanes = products[0].shape[1] // 2
    for h in range(HALVES):
        for k, msg in zip(ORDER, recv):
            at = pl.ds(pl.multiple_of(h * work + (g ^ k) * group, CENTER_ROWS), group)
            a_ref[at, :] = msg[h * group : (h + 1) * group, :]
        tail = jnp.concatenate([mid[h * boxes : (h + 1) * boxes], pad], 0).astype(BF)
        a_ref[(h + 1) * work - CENTER_ROWS : (h + 1) * work, :] = tail
    a = a_ref[...]
    for i, k in enumerate(ORDER):
        product = jnp.dot(a, w_ref[g ^ k], preferred_element_type=F32)
        for h in range(HALVES):
            out = products[h * size + i]
            out[...] = product[h * work : h * work + out.shape[0]]
    rows = HALVES * group
    for k, msg in zip(ORDER, recv):
        cot = [msg[rows:, i * lanes : (i + 1) * lanes] for i in range(depth // lanes)]
        cot = jnp.concatenate(cot, 0)
        low, high = cot[:rows], cot[rows:]
        for ref, value in (
            (keep_ref, jnp.where(c == 0, low, high)),
            (send_ref, jnp.where(c == 0, high, low)),
        ):
            for h in range(HALVES):
                at = pl.ds(pl.multiple_of(h * size * group + (g ^ k) * group, group), group)
                ref[at, :] = value[h * group : (h + 1) * group]


def relax_kernel(size, boxes, part, s_ref, *refs):
    g = s_ref[0]
    sums, (keep_ref, got_ref, own_ref, oth_ref), outs = refs[:size], refs[size : size + 4], refs[size + 4 :]
    back_ref, go_ref, msgs, out_scratch = outs[0], outs[1], outs[2:-1], outs[-1]
    pre = sums[0][...]
    for p in sums[1:]:
        pre = pre + p[...]
    group = go_ref.shape[0]
    rows, per = size * group, group // boxes
    cot = jnp.concatenate([keep_ref[...], got_ref[...]], 1).astype(F32)
    small = jnp.concatenate([own_ref[...], oth_ref[...]], 1)
    step = HALVES * boxes
    phase, center_cot, offset_cot = (
        small[i * step + part * boxes : i * step + (part + 1) * boxes] for i in range(3)
    )
    bias = small[3 * step : 3 * step + 1]
    where = [[q * group + b * per for q in range(size)] for b in range(boxes)]
    radius, cross = [], []
    for b in range(boxes):
        radius.append(sum(jnp.sum(jnp.abs(pre[r : r + per]), 0, keepdims=True) for r in where[b]))
        cross.append(sum(jnp.sum(cot[r : r + per] * pre[r : r + per], 0, keepdims=True) for r in where[b]))
    radius, cross = jnp.concatenate(radius, 0), jnp.concatenate(cross, 0)
    center_pre = pre[rows : rows + boxes] + bias
    (slope, center_out, offset), pull = jax.vjp(lambda a, b: neuron(a, b, phase), center_pre, radius)
    g_center, g_radius = pull((cross, center_cot, offset_cot))
    for b in range(boxes):
        sl, gr = slope[b : b + 1], g_radius[b : b + 1]
        for r in where[b]:
            x = pre[r : r + per]
            sign = jnp.where(x > 0, gr, jnp.where(x < 0, -gr, 0.0))
            back_ref[r : r + per, :] = (sl * cot[r : r + per] + sign).astype(BF)
            out_scratch[r : r + per, :] = (sl * x).astype(BF)
    tail = []
    for value in (g_center, center_out, offset):
        high = value.astype(BF).astype(F32)
        tail += [high, value - high]
    tail.append(jnp.zeros((CENTER_ROWS - 6 * boxes, value.shape[1]), F32))
    back_ref[rows:, :] = jnp.concatenate(tail, 0).astype(BF)
    go_ref[...] = out_scratch[rows_at(g, group), :]
    for k, msg in zip(BACK_ORDER[1:], msgs):
        msg[: rows + CENTER_ROWS, :] = back_ref[...]
        msg[rows + CENTER_ROWS :, :] = out_scratch[rows_at(g ^ k, group), :]


def spread_kernel(s_ref, back_ref, go_ref, *refs):
    g = s_ref[0]
    msgs, (own_ref, oth_ref, far_ref, out_ref) = refs[:3], refs[3:]
    rows, lanes = back_ref.shape[0], back_ref.shape[1] // 2
    for i, k in enumerate(BACK_ORDER):
        at = rows_at(g ^ k, lanes)
        back, out = (back_ref, go_ref[...]) if i == 0 else (msgs[i - 1], msgs[i - 1][rows:, :])
        own_ref[:, at] = back[:rows, :lanes]
        oth_ref[:rows, at] = back[:rows, lanes:]
        far_ref[:, at] = back[:rows, lanes:]
        oth_ref[rows:, at] = out[:, lanes:]
        out_ref[:, at] = out[:, :lanes]


def input_grad_kernel(s_ref, back_ref, *refs):
    g, c, x = s_ref[0], s_ref[1], s_ref[2] >> 1
    msgs, w_ref, outs, res = refs[:3], refs[3], refs[4:-1], refs[-1]
    rows = back_ref.shape[0]
    over = (((1,), (1,)), ((), ()))
    total = None
    for i, k in enumerate(BACK_ORDER):
        back = back_ref[...] if i == 0 else msgs[i - 1][:rows, :]
        part = lax.dot_general(back, w_ref[g ^ k], over, preferred_element_type=F32)
        total = part if total is None else total + part
    res[...] = total
    group = (rows - CENTER_ROWS) // 4
    tail = res[4 * group : 4 * group + 8, :]
    for side, out in ((1 - x, outs[0]), (x, outs[1])):
        first = res[rows_at(side + 2 * c, group), :]
        second = res[rows_at(side + 2 * (1 - c), group), :]
        out[...] = jnp.concatenate([first, second, tail], 0).astype(out.dtype)


def input_both_kernel(s_ref, keep_ref, far_ref, first_ref, last_ref):
    group = (keep_ref.shape[0] - 8) // 2
    total = keep_ref[...] + far_ref[...].astype(F32)
    tail = total[2 * group :]
    first_ref[...] = jnp.concatenate([total[:group], tail], 0).astype(BF)
    last_ref[...] = jnp.concatenate([total[group : 2 * group], tail], 0).astype(BF)


def input_final_kernel(boxes, s_ref, *refs):
    msgs, (grad_ref, center_ref) = refs[:-2], refs[-2:]
    first = s_ref[0] >> 1
    per = grad_ref.shape[1]
    group = boxes * per
    rows = [[], []]
    for h in range(HALVES):
        for k in range(2):
            value = msgs[k][h * (group + 8) : (h + 1) * (group + 8), :].astype(F32)
            at = (first ^ k) * (HALVES * boxes) + h * boxes
            grad_ref[pl.ds(at, boxes)] = value[:group].reshape(boxes, per, -1)
            rows[k].append(value[group : group + boxes])
    near, far = (jnp.concatenate(r, 0) for r in rows)
    center_ref[...] = jnp.where(
        first == 0, jnp.concatenate([near, far], 0), jnp.concatenate([far, near], 0)
    )


def stack_kernel(s_ref, *refs):
    lefts, out = refs[:-1], refs[-1]
    rows = lefts[0].shape[0] // HALVES
    gens = rows - CENTER_ROWS
    tails = []
    for i in range(len(lefts) * HALVES):
        ref, h = lefts[i // HALVES], i % HALVES
        out[:, i * gens : (i + 1) * gens] = ref[h * rows : h * rows + gens, :].T
        tails.append(ref[h * rows + gens : (h + 1) * rows, :])
    width = out.shape[1] - len(lefts) * HALVES * gens
    pad = jnp.zeros((width - len(tails) * CENTER_ROWS, out.shape[0]), BF)
    out[:, len(tails) * gens :] = jnp.concatenate(tails + [pad], 0).T


def weight_grad_kernel(boxes, s_ref, after_ref, left_ref, *refs):
    rights, keeps, refs = refs[: 4 * HALVES], refs[4 * HALVES : 5 * HALVES], refs[5 * HALVES :]
    weight_ref, bias_ref, center_ref, offset_ref, gens_ref, done_ref, stack = refs
    per = gens_ref.shape[1]
    cols = weight_ref.shape[1]
    gens = rights[-1].shape[0] - CENTER_ROWS

    @pl.when(pl.program_id(0) == 0)
    def _():
        c = s_ref[1]
        done_ref[...] = jnp.zeros(done_ref.shape, F32)
        tails = []
        for i, right in enumerate(rights):
            tail = right[gens : gens + CENTER_ROWS, :cols]
            stack[i * CENTER_ROWS : (i + 1) * CENTER_ROWS, :] = tail
            tails.append(tail.astype(F32))
        used = len(rights) * CENTER_ROWS
        stack[used:, :] = jnp.zeros((stack.shape[0] - used, cols), BF)
        bias_ref[...] = sum(jnp.sum(t[: 2 * boxes], 0, keepdims=True) for t in tails)
        for at, ref in ((2, center_ref), (4, offset_ref)):
            both = [
                t[at * boxes : (at + 1) * boxes] + t[(at + 1) * boxes : (at + 2) * boxes]
                for t in tails[: 2 * HALVES]
            ]
            mine, other = (jnp.concatenate(both[i * HALVES : (i + 1) * HALVES], 0) for i in range(2))
            ref[...] = jnp.where(
                c == 0, jnp.concatenate([mine, other], 0), jnp.concatenate([other, mine], 0)
            )
        for h in range(HALVES):
            for at, out in ((c, keeps[h][...]), (1 - c, rights[HALVES + h][gens + CENTER_ROWS :, :])):
                at = at * (HALVES * boxes) + h * boxes
                gens_ref[pl.ds(at, boxes)] = out.reshape(boxes, per, -1)

    total = jnp.dot(left_ref[:, len(rights) * gens :], stack[...], preferred_element_type=F32)
    for i, right in enumerate(rights):
        part = left_ref[:, i * gens : (i + 1) * gens]
        total += jnp.dot(part, right[:gens, :cols], preferred_element_type=F32)
    weight_ref[...] = total


def square_body(size, gens, center, weight, bias, phase, gens_cot, center_cot, offset_cot):
    box_dev, per_gen, width = gens.shape
    depth, cols = weight.shape
    core_boxes = box_dev // 2
    boxes = core_boxes // HALVES
    group = boxes * per_gen
    rows = size * group
    work = rows + CENTER_ROWS
    lanes = cols // size
    g, n = lax.axis_index("gen"), lax.axis_index("neur")
    c = n % 2
    scalars = jnp.stack([g, c, n, lax.axis_index("box")]).astype(jnp.int32)
    halves = range(HALVES)

    def over_gen(pieces, order=ORDER):
        return [pieces[0]] + [
            lax.ppermute(piece, "gen", [(i, i ^ k) for i in range(size)])
            for piece, k in zip(pieces[1:], order[1:])
        ]

    def over_core(x):
        return lax.ppermute(x, "neur", [(i, i ^ 1) for i in range(size)])

    def over_x(x):
        return lax.ppermute(x, "neur", [(i, i ^ 2) for i in range(size)])

    def over_box(x):
        return lax.ppermute(x, "box", [(0, 1), (1, 0)])

    def over_both(x):
        pairs = [(i * 2 + j, (i ^ 1) * 2 + (j ^ 1)) for i in range(size) for j in range(2)]
        return lax.ppermute(x, ("neur", "box"), pairs)

    def turned(x, k):
        pairs = [
            (i * size + j, ((j >> 1) + 2 * ((j & 1) ^ k)) * size + i)
            for i in range(size)
            for j in range(size)
        ]
        return lax.ppermute(x, ("gen", "neur"), pairs)

    anywhere = pl.BlockSpec(memory_space=pl.ANY)
    def held(x, *after):
        if not after:
            return x
        return call(copy_kernel, scalars, [x], [whole(x)], [shape(x.shape, x.dtype)], after=after)[0]

    with jax.named_scope("exchange_generators"):
        cot_rows = box_dev * per_gen * lanes // depth
        msgs = call(
            functools.partial(fold_kernel, size),
            scalars,
            [gens, gens_cot],
            [anywhere] * 2,
            [shape((core_boxes * per_gen + cot_rows, depth), BF)] * size,
            [pltpu.VMEM(gens_cot.shape, BF), pltpu.SemaphoreType.DMA((size * core_boxes + 1,))],
        )
        recv = over_gen(msgs)
    with jax.named_scope("swap_cores"):
        w_other = over_core(weight)
        (w_chunks,) = call(
            chunk_kernel,
            scalars,
            [weight, w_other],
            [whole(weight), whole(w_other)],
            [shape((size, depth, 2 * lanes), BF)],
            after=[recv[1]],
        )
        stacked = jnp.stack([phase.astype(F32), center_cot, offset_cot])

        def small(core):
            part = lax.dynamic_slice_in_dim(stacked, core * core_boxes, core_boxes, 1)
            pad = jnp.zeros((8 - 3 * core_boxes - 1, cols), F32)
            return jnp.concatenate([part.reshape(3 * core_boxes, cols), bias[None], pad], 0)

        small_own = small(c)
        small_oth = over_core(small(1 - c))
    with jax.named_scope("forward"):
        a_own, cot_keep, cot_send, *products = call(
            functools.partial(forward_kernel, size),
            scalars,
            [center, w_chunks, *recv],
            [
                pl.BlockSpec((box_dev, depth), lambda i, s: (0, s[0])),
                whole(w_chunks),
                *[whole(r) for r in recv],
            ],
            [shape((HALVES * work, depth), BF)]
            + [shape((HALVES * rows, lanes), BF)] * 2
            + [shape((rows + 8, 2 * lanes), F32)] * (HALVES * size),
        )
    with jax.named_scope("sum_products"):
        sums = []
        for h in halves:
            sums.append(over_gen(products[h * size : (h + 1) * size]))
        cot_got = over_core(cot_send)
    with jax.named_scope("share_generators"):
        a_box = over_box(a_own)
        pieces = [a_own, over_core(a_own), a_box, over_core(a_box)]
        (left,) = call(
            stack_kernel,
            scalars,
            pieces,
            [whole(v) for v in pieces],
            [shape((depth, 4 * HALVES * rows + 128), BF)],
        )
    keeps, sends = [], []
    small_spec = pl.BlockSpec((8, lanes), lambda i, s: (0, s[0]))
    for h in halves:
        cot_part = pl.BlockSpec((rows, lanes), lambda i, s, h=h: (h, 0))
        with jax.named_scope("relax"):
            back, go, *msgs = call(
                functools.partial(relax_kernel, size, boxes, h),
                scalars,
                [*sums[h], cot_keep, cot_got, small_own, small_oth],
                [*[whole(p) for p in sums[h]], cot_part, cot_part, small_spec, small_spec],
                [
                    shape((work, 2 * lanes), BF),
                    shape((group, 2 * lanes), BF),
                    *[shape((work + group, 2 * lanes), BF)] * (size - 1),
                ],
                [pltpu.VMEM((rows, 2 * lanes), BF)],
            )
        with jax.named_scope("exchange_back"):
            got = over_gen([None, *msgs], BACK_ORDER)[1:]
            both = group + 8
            part = group + both
            send, keep = call(
                input_grad_kernel,
                scalars,
                [back, *got, w_chunks],
                [whole(v) for v in (back, *got, w_chunks)],
                [shape((part, depth), BF), shape((part, depth), F32)],
                [pltpu.VMEM((work, depth), F32)],
            )
            own, oth, oth_back, out_own = call(
                spread_kernel,
                scalars,
                [back, go, *got],
                [whole(v) for v in (back, go, *got)],
                [
                    shape((work, cols), BF),
                    shape((work + group, cols), BF),
                    shape((work, cols), BF),
                    shape((group, cols), BF),
                ],
                after=[send],
            )
            core_part = over_core(oth)
            keeps.append(out_own)
    with jax.named_scope("input_gradient"):

        far = over_x(send)
        first, last = call(
            input_both_kernel,
            scalars,
            [keep, far],
            [whole(keep), whole(far)],
            [shape((both, depth), BF)] * 2,
        )
        finals = [turned(first, 0), turned(last, 1)]
        rights = [own, core_part, over_box(own), held(over_both(oth_back), last)]
    with jax.named_scope("weight_gradient"):
        blocks = 4
        out_shape = [
            shape((depth, cols), F32),
            shape((1, cols), F32),
            shape((box_dev, cols), F32),
            shape((box_dev, cols), F32),
            shape((box_dev, per_gen, cols), BF),
            shape((8, 128), F32),
        ]
        weight_grad, bias_grad, center_out, offset, gens_out, done = pl.pallas_call(
            functools.partial(weight_grad_kernel, boxes),
            grid_spec=pltpu.PrefetchScalarGridSpec(
                num_scalar_prefetch=1,
                grid=(blocks,),
                in_specs=[anywhere, pl.BlockSpec((depth // blocks, left.shape[1]), lambda i, s: (i, 0))]
                + [whole(r) for r in rights + keeps],
                out_specs=[pl.BlockSpec((depth // blocks, cols), lambda i, s: (i, 0))]
                + [whole(o) for o in out_shape[1:]],
                scratch_shapes=[pltpu.VMEM((128, cols), BF)],
            ),
            out_shape=out_shape,
            compiler_params=params(),
        )(scalars, last, left, *rights, *keeps)
    with jax.named_scope("input_gradient"):
        gens_grad, center_grad = call(
            functools.partial(input_final_kernel, boxes),
            scalars,
            finals,
            [whole(r) for r in finals],
            [shape((box_dev, per_gen, depth), F32), shape((box_dev, depth), F32)],
            after=[done],
        )
    return (
        center_out,
        gens_out,
        offset,
        weight_grad,
        bias_grad.reshape(cols),
        gens_grad,
        center_grad,
    )


def solution(mesh):
    sizes = dict(mesh.shape)

    def run(gens, center, weight, bias, phase, gens_cot, center_cot, offset_cot):
        size = sizes["gen"]
        box_dev = gens.shape[0] // sizes["box"]
        per_gen = gens.shape[1] // size
        cols = weight.shape[1] // sizes["neur"]
        square = (
            size == sizes["neur"] == 4
            and sizes["box"] == 2
            and box_dev == 4
            and per_gen % 16 == 0
            and cols % (128 * size) == 0
            and weight.shape[0] % (1024 * size) == 0
        )
        body = functools.partial(square_body, size) if square else general_body
        return jax.shard_map(
            body,
            mesh=mesh,
            in_specs=(
                P("box", "gen", None),
                P("box", None),
                P("gen", "neur"),
                P("neur"),
                P("box", "neur"),
                P("box", "gen", "neur"),
                P("box", "neur"),
                P("box", "neur"),
            ),
            out_specs=(
                P("box", "neur"),
                P("box", "gen", "neur"),
                P("box", "neur"),
                P("gen", "neur"),
                P("neur"),
                P("box", "gen", "neur"),
                P("box", "neur"),
            ),
            check_vma=False,
        )(gens, center, weight, bias, phase, gens_cot, center_cot, offset_cot)

    return run
```
